32 devices in a mesh: ctx: 4 (over y, x), mp: 8 (over z, core).
Axes of the slice: x: 2, y: 2, z: 4, core: 2. Of those that a mesh axis runs over, the one named last changes fastest.
Arguments:
- residual_in: bfloat16 [2048, 8192], P('ctx', 'mp'), may hold values from -4 to 4
- query_rows: bfloat16 [2048, 8192], P('ctx', 'mp'), may hold values from -5 to 5
- key_rows: bfloat16 [2048, 8192], P('ctx', 'mp'), may hold values from -5 to 5
- value_rows: bfloat16 [2048, 8192], P('ctx', 'mp'), may hold values from -5 to 5
- out_weight: bfloat16 [8192, 8192], P('mp'), may hold values from -0.75 to 0.75
- gate_in: bfloat16 [2048, 8192], P('ctx', 'mp'), may hold values from -5 to 5
- gate_out: bfloat16 [2048, 8192], P('ctx', 'mp'), may hold values from -5 to 5
- short_taps: float32 [3, 8192], P(None, 'mp'), may hold values from -3 to 3
- decay_rates: float32 [16, 8192], P(None, 'mp'), may hold values from 9.765625e-05 to 0.03
- residues: float32 [16, 8192], P(None, 'mp'), may hold values from -0.15 to 0.15
- skip_gain: float32 [8192], P('mp'), may hold values from -4 to 4
Outputs:
- attended: bfloat16 [2048, 8192], P('ctx', 'mp')
- hyena_out: bfloat16 [2048, 8192], P('ctx', 'mp')
The draws below stay inside these ranges and needn't reach their ends.
All inputs are finite; a program needn't handle non-finite values.
Results may differ from the reference program's by a relative error of at most 0.02.
Values may be sent and summed in bfloat16 or wider, within the bound.
A program may use at most 128 MiB of HBM per device.

```python
import math
import jax
import jax.numpy as jnp
from jax import lax

D = 8192
HEADS = 64
HD = 128
POLES = 16
TAPS = 3
BLOCK = 64
SEQ = 2048
N_MP = 8


def drawn_rows(key, salt):
    sub = jax.random.fold_in(key, salt)
    return jnp.clip(jax.random.normal(sub, (SEQ, HEADS * HD), jnp.float32), -5.0, 5.0)


def draw_query_rows(key, part):
    drawn = drawn_rows(key, 1)
    return drawn.astype(jnp.bfloat16)


def draw_key_rows(key, part):
    drawn = drawn_rows(key, 2)
    return drawn.astype(jnp.bfloat16)


def with_spikes(values, own_key, source, target, blocks, factor):
    def block_of(dim):
        return (jnp.arange(values.shape[dim]) // (values.shape[dim] // blocks)).reshape((-1,) + (1,) * (values.ndim - 1 - dim))

    one_side = jax.random.permutation(own_key, blocks)[block_of(target)]
    second = (block_of(target) + blocks // 2) % blocks
    return jnp.where((block_of(source) == one_side) | (block_of(source) == second), factor * values, values)


def level_of(own_key, extent, shards, smallest, high):
    loudness = 1.0
    for dim, blocks in shards:
        heights = jax.random.uniform(jax.random.fold_in(jax.random.fold_in(own_key, 6), dim), (blocks,), jnp.float32, smallest / len(shards), high / len(shards))
        loudness = loudness * jnp.repeat(jnp.exp(heights), extent[dim] // blocks).reshape((-1,) + (1,) * (len(extent) - 1 - dim))
    return loudness


def normal_values(own_key, dims, scale, bound, cuts=(), held_as=jnp.bfloat16):
    loudness = level_of(own_key, dims, cuts, -0.22, 0.18) if cuts else 1.0
    drawn = jax.random.normal(own_key, dims, jnp.float32) * scale * loudness
    return jnp.minimum(jnp.maximum(drawn, -bound), bound).astype(held_as)


def heavy_noise(rng, dims, spread, bound, split, heavy, kind=jnp.bfloat16):
    values = spread * jax.random.normal(rng, dims, jnp.float32)
    if split:
        values = values * level_of(rng, dims, split, -0.22, 0.18)
    return jnp.clip(with_spikes(values, jax.random.fold_in(rng, 3), *heavy), -bound, bound).astype(kind)


def setup_inputs(seed: int = 0) -> dict:
    key_of = jax.random.split(jax.random.key(seed), 12)
    residual_in = normal_values(key_of[0], (SEQ, D), 0.5, 4.0, ((0, 4), (1, 8)))
    query_rows = draw_query_rows(jax.random.fold_in(key_of[11], 71), 0)
    key_rows = draw_key_rows(jax.random.fold_in(key_of[11], 71), 0)
    value_rows = normal_values(key_of[3], (SEQ, HEADS * HD), 1.0, 5.0, ((0, 4), (1, 8)))
    out_weight = heavy_noise(key_of[4], (HEADS * HD, D), HD ** -0.5, 0.75, ((0, 8),), (0, 1, 8, 2.0))
    gate_in = normal_values(key_of[5], (SEQ, D), 1.0, 5.0, ((0, 4), (1, 8)))
    gate_out = normal_values(key_of[6], (SEQ, D), 1.0, 5.0, ((0, 4), (1, 8)))
    short_taps = normal_values(key_of[7], (TAPS, D), 0.6, 3.0, ((1, 8),), jnp.float32)
    decay_rates = jnp.clip(jnp.exp(math.log(0.03) - 5.727499 * jax.random.uniform(key_of[8], (POLES, D), jnp.float32) ** level_of(key_of[8], (POLES, D), ((1, 8),), -0.2, 0.2)), 9.765625145519152e-05, 0.03)
    residues = normal_values(key_of[9], (POLES, D), 0.03, 0.15, ((1, 8),), jnp.float32)
    skip_gain = normal_values(key_of[10], (D,), 1.0, 4.0, ((0, 8),), jnp.float32)
    return {"residual_in": residual_in, "query_rows": query_rows, "key_rows": key_rows, "value_rows": value_rows, "out_weight": out_weight, "gate_in": gate_in, "gate_out": gate_out, "short_taps": short_taps, "decay_rates": decay_rates, "residues": residues, "skip_gain": skip_gain}


masked_floor = -1e30


def head_attention(query_head, key_head, value_head):
    scores = jnp.dot(query_head, key_head.T, preferred_element_type=jnp.float32) * (HD ** -0.5)
    positions = jnp.arange(SEQ)
    allowed = positions[None, :] <= positions[:, None]
    masked = jnp.where(allowed, scores, masked_floor)
    highest = jnp.max(masked, axis=1, keepdims=True)
    weights = jnp.where(allowed, jnp.exp(masked - highest), 0.0)
    total = jnp.sum(weights, axis=1, keepdims=True)
    summed = jnp.dot(weights.astype(jnp.bfloat16), value_head, preferred_element_type=jnp.float32)
    return summed / total


def modal_tables(decay_rates, residues, block):
    width = decay_rates.shape[1]
    lags = jnp.arange(block).astype(jnp.float32)
    lag_diff = lags[:, None] - lags[None, :]
    causal = lag_diff >= 0
    safe_diff = jnp.maximum(lag_diff, 0.0)

    def add_pole(total, pole):
        rate, residue = pole
        return total + residue[None, None, :] * jnp.exp(-rate[None, None, :] * safe_diff[:, :, None]), None

    toeplitz, _ = lax.scan(add_pole, jnp.zeros((block, block, width), jnp.float32), (decay_rates, residues))
    toeplitz = jnp.where(causal[:, :, None], toeplitz, 0.0)
    powers = jnp.exp(-decay_rates[None] * lags[:, None, None])
    inward = jnp.exp(-decay_rates[None] * (block - lags)[:, None, None])
    return toeplitz, powers, inward


def modal_conv(signal, decay_rates, residues, block):
    length, width = signal.shape
    toeplitz, powers, inward = modal_tables(decay_rates, residues, block)
    highest = lax.Precision.HIGHEST
    span = jnp.exp(-decay_rates * block)

    def step(state, piece):
        local = jnp.einsum('ijc,jc->ic', toeplitz, piece, precision=highest)
        carried = jnp.einsum('inc,nc->ic', powers, residues * state, precision=highest)
        state = span * state + jnp.einsum('jnc,jc->nc', inward, piece, precision=highest)
        return state, local + carried

    start_state = jnp.zeros((decay_rates.shape[0], width), jnp.float32)
    state, result = lax.scan(step, start_state, signal.reshape(length // block, block, width))
    return result.reshape(length, width), state


def reference(residual_in, query_rows, key_rows, value_rows, out_weight, gate_in, gate_out, short_taps, decay_rates, residues, skip_gain):
    def by_head(arr):
        return arr.reshape(SEQ, HEADS, HD).transpose(1, 0, 2)

    heads_out = lax.map(lambda trio: head_attention(trio[0], trio[1], trio[2]), (by_head(query_rows), by_head(key_rows), by_head(value_rows)))
    heads_out = heads_out.transpose(1, 0, 2).reshape(SEQ, HEADS * HD).astype(jnp.bfloat16)
    group_cols = HEADS * HD // N_MP
    head_groups = heads_out.reshape(SEQ, N_MP, group_cols).transpose(1, 0, 2)
    weight_groups = out_weight.reshape(N_MP, group_cols, D)

    def add_group(total, pair):
        partial_sum = jnp.dot(pair[0], pair[1], preferred_element_type=jnp.float32)
        rounded = lax.optimization_barrier(partial_sum.astype(jnp.bfloat16))
        return total + rounded.astype(jnp.float32), None

    projected, _ = lax.scan(add_group, jnp.zeros((SEQ, D), jnp.float32), (head_groups, weight_groups))
    attended = (residual_in.astype(jnp.float32) + projected).astype(jnp.bfloat16)
    stream = attended.astype(jnp.float32)
    padded = jnp.concatenate([jnp.zeros((TAPS - 1, D), jnp.float32), stream], axis=0)
    shortconv = jnp.zeros((SEQ, D), jnp.float32)
    for tap in range(TAPS):
        shortconv = shortconv + short_taps[tap][None, :] * padded[TAPS - 1 - tap:TAPS - 1 - tap + SEQ]
    signal = gate_in.astype(jnp.float32) * shortconv
    longconv, _ = modal_conv(signal, decay_rates, residues, BLOCK)
    hyena_out = (gate_out.astype(jnp.float32) * (longconv + skip_gain[None, :] * signal)).astype(jnp.bfloat16)
    return attended, hyena_out
```

```python
import functools
import math

import jax
import jax.numpy as jnp
from jax import lax
from jax.experimental import pallas as pl
from jax.experimental.pallas import tpu as pltpu
from jax.sharding import PartitionSpec as P

HD = 128
LANES = 128
CHUNKS = 8
masked_floor = -1e30


def causal_attention_kernel(query_ref, key_ref, value_ref, out_ref):
    length = query_ref.shape[0]
    block = min(256, length)
    factor = HD ** (-0.5) * math.log2(math.e)
    row = lax.broadcasted_iota(jnp.int32, (block, block), 0)
    column = lax.broadcasted_iota(jnp.int32, (block, block), 1)
    contract_last = (((1,), (1,)), ((), ()))
    for start in range(0, length, block):
        queries = query_ref[start : start + block, :]
        diagonal = lax.dot_general(
            queries,
            key_ref[start : start + block, :],
            contract_last,
            preferred_element_type=jnp.float32,
        )
        diagonal = jnp.where(column <= row, diagonal, masked_floor)
        highest = jnp.max(diagonal, axis=1, keepdims=True)
        if start:
            earlier = lax.dot_general(
                queries, key_ref[:start, :], contract_last, preferred_element_type=jnp.float32
            )
            highest = jnp.maximum(highest, jnp.max(earlier, axis=1, keepdims=True))
        shift = highest * factor
        weights = jnp.exp2(diagonal * factor - shift)
        total = jnp.sum(weights, axis=1, keepdims=True)
        summed = jnp.dot(
            weights.astype(jnp.bfloat16),
            value_ref[start : start + block, :],
            preferred_element_type=jnp.float32,
        )
        if start:
            weights = jnp.exp2(earlier * factor - shift)
            total = total + jnp.sum(weights, axis=1, keepdims=True)
            summed = summed + jnp.dot(
                weights.astype(jnp.bfloat16),
                value_ref[:start, :],
                preferred_element_type=jnp.float32,
            )
        out_ref[start : start + block, :] = (summed / total).astype(jnp.bfloat16)


def causal_attention(queries, keys, values):
    length, width = queries.shape
    heads = width // HD
    spec = pl.BlockSpec((length, HD), lambda head: (0, head))
    return pl.pallas_call(
        causal_attention_kernel,
        grid=(heads,),
        in_specs=[spec] * 3,
        out_specs=spec,
        out_shape=jax.ShapeDtypeStruct((length, width), jnp.bfloat16),
        compiler_params=pltpu.CompilerParams(vmem_limit_bytes=48 * 1024 * 1024),
        cost_estimate=pl.CostEstimate(
            flops=2 * length * length * width,
            bytes_accessed=8 * length * width,
            transcendentals=heads * length * length // 2,
        ),
    )(queries, keys, values)


def from_behind(value, axis, steps):
    count = lax.axis_size(axis)
    leading, last = (max(0, -steps), min(count, count - steps))
    return lax.ppermute(value, axis, [(source, source + steps) for source in range(leading, last)])


def attend(groups, key_rows, value_rows):
    width = key_rows.shape[1]
    heads = width // HD
    scale = HD ** (-0.5)
    query_sets = [(rows_q.reshape(rows_q.shape[0], heads, HD), pos_q) for rows_q, pos_q in groups]

    def update(state, queries, query_pos, keys_here, values_here, key_pos):
        running_top, running_total, running_sum = state
        scores = (
            jnp.einsum("qhd,khd->hqk", queries, keys_here, preferred_element_type=jnp.float32)
            * scale
        )
        allowed = (key_pos[None, :] <= query_pos[:, None])[None]
        masked = jnp.where(allowed, scores, masked_floor)
        new_top = jnp.maximum(running_top, jnp.max(masked, axis=-1))
        weights = jnp.where(allowed, jnp.exp(masked - new_top[..., None]), 0.0)
        rescale = jnp.exp(running_top - new_top)
        new_total = running_total * rescale + jnp.sum(weights, axis=-1)
        new_sum = running_sum * rescale[..., None] + jnp.einsum(
            "hqk,khd->hqd",
            weights.astype(jnp.bfloat16),
            values_here,
            preferred_element_type=jnp.float32,
        )
        return (new_top, new_total, new_sum)

    initial = tuple(
        (
            (
                jnp.full((heads, pos_q.shape[0]), masked_floor, jnp.float32),
                jnp.zeros((heads, pos_q.shape[0]), jnp.float32),
                jnp.zeros((heads, pos_q.shape[0], HD), jnp.float32),
            )
            for rows_q, pos_q in groups
        )
    )
    pieces = (
        lax.all_gather(key_rows, "ctx", axis=0, tiled=True),
        lax.all_gather(value_rows, "ctx", axis=0, tiled=True),
    )
    count = pieces[0].shape[0]
    blocks = count // count
    keys_all = pieces[0].reshape(blocks, count, heads, HD)
    values_all = pieces[1].reshape(blocks, count, heads, HD)
    index_rows = jnp.arange(count)
    pos_all = index_rows.reshape(blocks, count)

    def fold_step(states, block):
        keys_here, values_here, key_pos = block
        return (
            tuple(
                (
                    update(
                        states[g],
                        query_sets[g][0],
                        query_sets[g][1],
                        keys_here,
                        values_here,
                        key_pos,
                    )
                    for g in range(len(query_sets))
                )
            ),
            None,
        )

    result, _ = lax.scan(fold_step, initial, (keys_all, values_all, pos_all))
    return [(final[2] / final[1][..., None]).astype(jnp.bfloat16) for final in result]

def recurrence_states(signal_ref, rates_ref, ends_ref, state_ref):
    rows = signal_ref.shape[0]
    poles = rates_ref.shape[0]
    step = rows // CHUNKS
    decays = [
        jnp.broadcast_to(jnp.exp(-rates_ref[n : n + 1, :]), (CHUNKS, LANES)) for n in range(poles)
    ]

    def advance(i, states):
        piece = signal_ref[pl.ds(i, CHUNKS, stride=step), :]
        return tuple(decay * state + piece for decay, state in zip(decays, states))

    start = tuple(jnp.zeros((CHUNKS, LANES), jnp.float32) for _ in range(poles))
    ends = lax.fori_loop(0, step, advance, start, unroll=4)
    for n in range(poles):
        ends_ref[:, n, :] = ends[n]
    span = jnp.exp(-rates_ref[...] * float(step))
    total = jnp.zeros((poles, LANES), jnp.float32)
    for chunk in range(CHUNKS):
        total = span * total + ends_ref[chunk]
    state_ref[...] = total


def recurrence_outputs(signal_ref, rates_ref, residues_ref, ends_ref, before, conv_ref):
    rows = signal_ref.shape[0]
    poles = rates_ref.shape[0]
    step = rows // CHUNKS
    span = jnp.exp(-rates_ref[...] * float(step))
    for chunk in range(CHUNKS):
        here = ends_ref[chunk]
        ends_ref[chunk] = before
        before = span * before + here
    decays = [
        jnp.broadcast_to(jnp.exp(-rates_ref[n : n + 1, :]), (CHUNKS, LANES)) for n in range(poles)
    ]
    weights = [jnp.broadcast_to(residues_ref[n : n + 1, :], (CHUNKS, LANES)) for n in range(poles)]

    def advance(i, states):
        rows_here = pl.ds(i, CHUNKS, stride=step)
        piece = signal_ref[rows_here, :]
        states = tuple(decay * state + piece for decay, state in zip(decays, states))
        terms = [weight * state for weight, state in zip(weights, states)]
        while len(terms) > 1:
            terms = [sum(terms[i : i + 2][1:], terms[i]) for i in range(0, len(terms), 2)]
        conv_ref[rows_here, :] = terms[0]
        return states

    lax.fori_loop(0, step, advance, tuple(ends_ref[:, n, :] for n in range(poles)), unroll=2)


def make_signal(attended_ref, rim_ref, gate_ref, taps_ref, stream_ref, signal_ref):
    rows = attended_ref.shape[0]
    taps = taps_ref.shape[0]
    pad = rim_ref.shape[0]
    stream_ref[:pad, :] = rim_ref[...].astype(jnp.float32)
    stream_ref[pad:, :] = attended_ref[...].astype(jnp.float32)
    mixed = taps_ref[0:1, :] * stream_ref[pad : pad + rows, :]
    for tap in range(1, taps):
        mixed = mixed + taps_ref[tap : tap + 1, :] * stream_ref[pad - tap : pad - tap + rows, :]
    signal_ref[...] = gate_ref[...].astype(jnp.float32) * mixed


def states_kernel(attended_ref, rim_ref, gate_ref, taps_ref, rates_ref, signal_ref, ends_ref, state_ref, stream_ref):
    make_signal(attended_ref, rim_ref, gate_ref, taps_ref, stream_ref, signal_ref)
    recurrence_states(signal_ref, rates_ref, ends_ref, state_ref)


def outputs_kernel(signal_ref, ends_ref, before_ref, rates_ref, residues_ref, skip_ref, gate_ref, out_ref, held_ref, conv_ref):
    held_ref[...] = ends_ref[...]
    recurrence_outputs(signal_ref, rates_ref, residues_ref, held_ref, before_ref[...], conv_ref)
    mixed = conv_ref[...] + skip_ref[...] * signal_ref[...]
    out_ref[...] = (gate_ref[...].astype(jnp.float32) * mixed).astype(jnp.bfloat16)


def by_lanes(rows):
    return pl.BlockSpec((rows, LANES), lambda g: (0, g))


def hyena(attended, gate_in, gate_out, short_taps, decay_rates, residues, skip_gain):
    rows, width = attended.shape
    taps = short_taps.shape[0]
    poles = decay_rates.shape[0]
    segment = lax.axis_index("ctx")
    groups = width // LANES
    pad = 16
    rim = from_behind(attended[rows - pad :], "ctx", 1)
    ends_spec = pl.BlockSpec((CHUNKS, poles, LANES), lambda g: (0, 0, g))
    signal, ends, state = pl.pallas_call(
        states_kernel,
        grid=(groups,),
        in_specs=[by_lanes(rows), by_lanes(pad), by_lanes(rows), by_lanes(taps), by_lanes(poles)],
        out_specs=[by_lanes(rows), ends_spec, by_lanes(poles)],
        out_shape=[
            jax.ShapeDtypeStruct((rows, width), jnp.float32),
            jax.ShapeDtypeStruct((CHUNKS, poles, width), jnp.float32),
            jax.ShapeDtypeStruct((poles, width), jnp.float32),
        ],
        scratch_shapes=[pltpu.VMEM((pad + rows, LANES), jnp.float32)],
    )(attended, rim, gate_in, short_taps, decay_rates)
    states = lax.all_gather(state, "ctx", axis=0)
    earlier = jnp.arange(states.shape[0])
    gap = jnp.maximum((segment - earlier - 1) * rows, 0).astype(jnp.float32)
    factor = jnp.where(
        (earlier < segment)[:, None, None], jnp.exp(-decay_rates[None] * gap[:, None, None]), 0.0
    )
    before = jnp.sum(factor * states, axis=0)
    return pl.pallas_call(
        outputs_kernel,
        grid=(groups,),
        in_specs=[
            by_lanes(rows), ends_spec, by_lanes(poles), by_lanes(poles), by_lanes(poles), by_lanes(1), by_lanes(rows),
        ],
        out_specs=by_lanes(rows),
        out_shape=jax.ShapeDtypeStruct((rows, width), jnp.bfloat16),
        scratch_shapes=[
            pltpu.VMEM((CHUNKS, poles, LANES), jnp.float32),
            pltpu.VMEM((rows, LANES), jnp.float32),
        ],
    )(signal, ends, before, decay_rates, residues, skip_gain[None], gate_out)


def per_device(
    residual_in,
    query_rows,
    key_rows,
    value_rows,
    out_weight,
    gate_in,
    gate_out,
    short_taps,
    decay_rates,
    residues,
    skip_gain,
):
    rows, width = residual_in.shape
    segments = lax.axis_size("ctx")
    heads = width // HD
    if heads % segments == 0:
        spread = functools.partial(
            lax.all_to_all, axis_name="ctx", split_axis=1, concat_axis=0, tiled=True
        )
        own_heads = causal_attention(spread(query_rows), spread(key_rows), spread(value_rows))
        heads_out = lax.all_to_all(own_heads, "ctx", split_axis=0, concat_axis=1, tiled=True)
    else:
        query_pos = lax.axis_index("ctx") * rows + jnp.arange(rows)
        heads_out = attend([(query_rows, query_pos)], key_rows, value_rows)[0]
        heads_out = heads_out.transpose(1, 0, 2).reshape(rows, width)
    projected = lax.psum_scatter(
        jnp.einsum("qk,kc->cq", heads_out, out_weight, preferred_element_type=jnp.float32).astype(
            jnp.bfloat16
        ),
        "mp",
        scatter_dimension=0,
        tiled=True,
    ).astype(jnp.float32)
    attended = (residual_in.astype(jnp.float32) + projected.T).astype(jnp.bfloat16)
    hyena_out = hyena(attended, gate_in, gate_out, short_taps, decay_rates, residues, skip_gain)
    return (attended, hyena_out)


def solution(mesh):
    in_specs = (
        P("ctx", "mp"),
        P("ctx", "mp"),
        P("ctx", "mp"),
        P("ctx", "mp"),
        P("mp", None),
        P("ctx", "mp"),
        P("ctx", "mp"),
        P(None, "mp"),
        P(None, "mp"),
        P(None, "mp"),
        P("mp"),
    )
    out_specs = (P("ctx", "mp"), P("ctx", "mp"))
    return jax.shard_map(
        per_device, mesh=mesh, in_specs=in_specs, out_specs=out_specs, check_vma=False
    )
```

```python
import functools
import math

import jax
import jax.numpy as jnp
from jax import lax
from jax.experimental import pallas as pl
from jax.experimental.pallas import tpu as pltpu
from jax.sharding import PartitionSpec as P

HD = 128
LANES = 128
CHUNKS = 8
masked_floor = -1e30

MESH = pl.DeviceIdType.MESH


def attend_block(query_ref, key_ref, value_ref, out_ref, start, block):
    factor = HD ** (-0.5) * math.log2(math.e)
    row = lax.broadcasted_iota(jnp.int32, (block, block), 0)
    column = lax.broadcasted_iota(jnp.int32, (block, block), 1)
    contract_last = (((1,), (1,)), ((), ()))
    queries = query_ref[start : start + block, :]
    diagonal = lax.dot_general(
        queries,
        key_ref[start : start + block, :],
        contract_last,
        preferred_element_type=jnp.float32,
    )
    diagonal = jnp.where(column <= row, diagonal, masked_floor)
    highest = jnp.max(diagonal, axis=1, keepdims=True)
    if start:
        earlier = lax.dot_general(
            queries, key_ref[:start, :], contract_last, preferred_element_type=jnp.float32
        )
        highest = jnp.maximum(highest, jnp.max(earlier, axis=1, keepdims=True))
    shift = highest * factor
    weights = jnp.exp2(diagonal * factor - shift)
    total = jnp.sum(weights, axis=1, keepdims=True)
    summed = jnp.dot(
        weights.astype(jnp.bfloat16),
        value_ref[start : start + block, :],
        preferred_element_type=jnp.float32,
    )
    if start:
        weights = jnp.exp2(earlier * factor - shift)
        total = total + jnp.sum(weights, axis=1, keepdims=True)
        summed = summed + jnp.dot(
            weights.astype(jnp.bfloat16), value_ref[:start, :], preferred_element_type=jnp.float32
        )
    out_ref[start : start + block, :] = (summed / total).astype(jnp.bfloat16)


def spread_attention_kernel(
    n, block, query_ref, key_ref, value_ref, out_ref,
    queries, keys, values, results, send, recv, own, back_send, back_recv, back_own,
):
    me = lax.axis_index("ctx")
    rows = query_ref.shape[0]
    heads = queries.shape[0]
    barrier = pltpu.get_barrier_semaphore()
    for p in range(1, n):
        pl.semaphore_signal(
            barrier, inc=1, device_id={"ctx": lax.rem(me + p, n)}, device_id_type=MESH
        )
    pl.semaphore_wait(barrier, n - 1)

    sources = (key_ref, query_ref, value_ref)
    slots = (keys, queries, values)
    my_rows = pl.ds(pl.multiple_of(me * rows, rows), rows)
    arrivals = []
    own_copies = []
    for head in range(heads):
        arrivals.append([])
        own_copies.append([])
        for t in range(3):
            for p in range(n):
                target = lax.rem(me + p, n)
                columns = pl.ds(pl.multiple_of((target * heads + head) * HD, HD), HD)
                source = sources[t].at[:, columns]
                landing = slots[t].at[head, my_rows, :]
                if p == 0:
                    copy = pltpu.make_async_copy(source, landing, own.at[head, t])
                    own_copies[head].append(copy)
                else:
                    copy = pltpu.make_async_remote_copy(
                        src_ref=source,
                        dst_ref=landing,
                        send_sem=send.at[head, t, p],
                        recv_sem=recv.at[head, t, p],
                        device_id={"ctx": target},
                        device_id_type=MESH,
                    )
                    arrivals[head].append(copy)
                copy.start()

    returned = []
    for head in range(heads):
        for copy in own_copies[head]:
            copy.wait()
        for copy in arrivals[head]:
            copy.wait_recv()
        columns = pl.ds(pl.multiple_of((me * heads + head) * HD, HD), HD)
        landing = out_ref.at[:, columns]
        for segment in range(n):
            for start in range(segment * rows, (segment + 1) * rows, block):
                attend_block(
                    queries.at[head], keys.at[head], values.at[head], results.at[head], start, block
                )
            source = results.at[head, pl.ds(segment * rows, rows), :]
            away = lax.rem(segment - me + n, n)

            @pl.when(away != 0)
            def _():
                pltpu.make_async_remote_copy(
                    src_ref=source,
                    dst_ref=landing,
                    send_sem=back_send.at[head, away],
                    recv_sem=back_recv.at[head, away],
                    device_id={"ctx": segment},
                    device_id_type=MESH,
                ).start()

            @pl.when(away == 0)
            def _():
                pltpu.make_async_copy(source, landing, back_own.at[head]).start()

    for head in range(heads):
        source = results.at[head, pl.ds(0, rows), :]
        landing = out_ref.at[:, pl.ds(0, HD)]
        pltpu.make_async_copy(source, landing, back_own.at[head]).wait()
        for p in range(1, n):
            copy = pltpu.make_async_remote_copy(
                src_ref=source,
                dst_ref=landing,
                send_sem=back_send.at[head, p],
                recv_sem=back_recv.at[head, p],
                device_id={"ctx": lax.rem(me + p, n)},
                device_id_type=MESH,
            )
            copy.wait_send()
            copy.wait_recv()
        for copy in arrivals[head]:
            copy.wait_send()


def spread_attention(query_rows, key_rows, value_rows):
    rows, width = query_rows.shape
    n = lax.axis_size("ctx")
    heads = width // HD // n
    length = n * rows
    whole = pltpu.VMEM((heads, length, HD), jnp.bfloat16)
    dma = pltpu.SemaphoreType.DMA
    return pl.pallas_call(
        functools.partial(spread_attention_kernel, n, min(256, rows)),
        in_specs=[pl.BlockSpec(memory_space=pl.ANY)] * 3,
        out_specs=pl.BlockSpec(memory_space=pl.ANY),
        out_shape=jax.ShapeDtypeStruct((rows, width), jnp.bfloat16),
        scratch_shapes=[
            whole, whole, whole, whole,
            dma((heads, 3, n)), dma((heads, 3, n)), dma((heads, 3)),
            dma((heads, n)), dma((heads, n)), dma((heads,)),
        ],
        compiler_params=pltpu.CompilerParams(
            collective_id=1, has_side_effects=True, vmem_limit_bytes=48 * 1024 * 1024
        ),
        cost_estimate=pl.CostEstimate(
            flops=2 * length * length * heads * HD,
            bytes_accessed=8 * rows * width,
            transcendentals=heads * length * length // 2,
        ),
    )(query_rows, key_rows, value_rows)


def project_reduce_kernel(
    heads_ref, residual_ref, weight_ref, out_ref,
    weights, for_pair, from_pair, sums, from_end, from_mid,
    weight_sem, pair_send, pair_recv, end_send, end_recv, mid_send, mid_recv, back_send,
):
    mp = lax.axis_index("mp")
    core = lax.rem(mp, 2)
    chip = mp // 2
    mirrored = chip >= 2
    middle = jnp.logical_or(chip == 1, chip == 2)
    step = jnp.where(mirrored, -1, 1)
    pair = chip * 2 + 1 - core
    toward = (chip + step) * 2 + core
    behind = (chip - step) * 2 + core
    rows, width = residual_ref.shape
    parts = end_send.shape[1]
    part = rows // parts
    tile = min(256, width)

    copies = []
    for k in range(4):
        target = jnp.where(mirrored, k, 3 - k)
        for mine in range(2):
            owner = target * 2 + (core if mine else 1 - core)
            columns = pl.ds(pl.multiple_of(owner * width, width), width)
            copy = pltpu.make_async_copy(
                weight_ref.at[:, columns], weights.at[k, mine], weight_sem.at[k, mine]
            )
            copy.start()
            copies.append(copy)

    barrier = pltpu.get_barrier_semaphore()
    pl.semaphore_signal(barrier, inc=1, device_id={"mp": pair}, device_id_type=MESH)
    pl.semaphore_signal(barrier, inc=1, device_id={"mp": toward}, device_id_type=MESH)

    @pl.when(middle)
    def _():
        pl.semaphore_signal(barrier, inc=1, device_id={"mp": behind}, device_id_type=MESH)
        pl.semaphore_wait(barrier, 3)

    @pl.when(jnp.logical_not(middle))
    def _():
        pl.semaphore_wait(barrier, 2)

    def part_copy(source, landing, slot, h, send_sem, recv_sem, device):
        piece = pl.ds(h * part, part)
        return pltpu.make_async_remote_copy(
            src_ref=sums.at[source, piece, :],
            dst_ref=landing.at[slot, piece, :],
            send_sem=send_sem,
            recv_sem=recv_sem,
            device_id={"mp": device},
            device_id_type=MESH,
        )

    def to_middle(k, h):
        return part_copy(k, from_end, k, h, end_send.at[k, h], end_recv.at[k, h], toward)

    def across(k, h):
        return part_copy(k, from_mid, k, h, mid_send.at[k, h], mid_recv.at[k, h], toward)

    def to_end(h):
        return part_copy(3, from_mid, 0, h, back_send.at[h], mid_recv.at[0, h], behind)

    pair_copies = []
    for k in range(4):
        copies[2 * k].wait()

        @pl.loop(0, width // tile)
        def _(j):
            columns = pl.ds(pl.multiple_of(j * tile, tile), tile)
            for_pair[k, :, columns] = jnp.dot(
                heads_ref[...], weights[k, 0, :, columns], preferred_element_type=jnp.float32
            ).astype(jnp.bfloat16)

        copy = pltpu.make_async_remote_copy(
            src_ref=for_pair.at[k],
            dst_ref=from_pair.at[k],
            send_sem=pair_send.at[k],
            recv_sem=pair_recv.at[k],
            device_id={"mp": pair},
            device_id_type=MESH,
        )
        copy.start()
        pair_copies.append(copy)
        copies[2 * k + 1].wait()
        copy.wait_recv()

        @pl.loop(0, width // tile)
        def _(j):
            columns = pl.ds(pl.multiple_of(j * tile, tile), tile)
            mixed = jnp.dot(
                heads_ref[...], weights[k, 1, :, columns], preferred_element_type=jnp.float32
            )
            sums[k, :, columns] = (mixed + from_pair[k, :, columns].astype(jnp.float32)).astype(
                jnp.bfloat16
            )

        if k < 3:

            @pl.when(jnp.logical_not(middle))
            def _():
                for h in range(parts):
                    to_middle(k, h).start()

    def add(k, h, landing, slot):
        piece = pl.ds(h * part, part)
        total = sums[k, piece, :].astype(jnp.float32) + landing[slot, piece, :].astype(jnp.float32)
        sums[k, piece, :] = total.astype(jnp.bfloat16)

    def finish(h, k, landings):
        piece = pl.ds(h * part, part)
        total = sums[k, piece, :].astype(jnp.float32)
        for landing, slot in landings:
            total = total + landing[slot, piece, :].astype(jnp.float32)
        out_ref[piece, :] = (residual_ref[piece, :].astype(jnp.float32) + total).astype(jnp.bfloat16)

    @pl.when(middle)
    def _():
        for k in range(2):
            for h in range(parts):
                to_middle(k, h).wait_recv()
                add(k, h, from_end, k)
                across(k, h).start()
        for h in range(parts):
            across(0, h).wait_recv()
            add(3, h, from_mid, 0)
            to_end(h).start()
        for h in range(parts):
            to_middle(2, h).wait_recv()
            across(1, h).wait_recv()
            finish(h, 2, ((from_end, 2), (from_mid, 1)))
        for h in range(parts):
            across(0, h).wait_send()
            across(1, h).wait_send()
            to_end(h).wait_send()

    @pl.when(jnp.logical_not(middle))
    def _():
        for h in range(parts):
            across(0, h).wait_recv()
            finish(h, 3, ((from_mid, 0),))
        for k in range(3):
            for h in range(parts):
                to_middle(k, h).wait_send()

    for copy in pair_copies:
        copy.wait_send()


def project_reduce(heads_out, residual_in, out_weight):
    rows, width = residual_in.shape
    depth = heads_out.shape[1]
    parts = 4 if rows % 64 == 0 else 1
    vmem = pl.BlockSpec(memory_space=pltpu.VMEM)
    dma = pltpu.SemaphoreType.DMA

    def blocks(count):
        return pltpu.VMEM((count, rows, width), jnp.bfloat16)

    return pl.pallas_call(
        project_reduce_kernel,
        in_specs=[vmem, vmem, pl.BlockSpec(memory_space=pl.ANY)],
        out_specs=vmem,
        out_shape=jax.ShapeDtypeStruct((rows, width), jnp.bfloat16),
        scratch_shapes=[
            pltpu.VMEM((4, 2, depth, width), jnp.bfloat16),
            blocks(4), blocks(4), blocks(4), blocks(3), blocks(2),
            dma((4, 2)), dma((4,)), dma((4,)),
            dma((3, parts)), dma((3, parts)), dma((2, parts)), dma((2, parts)), dma((parts,)),
        ],
        compiler_params=pltpu.CompilerParams(
            collective_id=2, has_side_effects=True, vmem_limit_bytes=56 * 1024 * 1024
        ),
        cost_estimate=pl.CostEstimate(
            flops=16 * rows * depth * width,
            bytes_accessed=16 * depth * width + 6 * rows * width,
            transcendentals=0,
        ),
    )(heads_out, residual_in, out_weight)


def from_behind(value, axis, steps):
    count = lax.axis_size(axis)
    leading, last = (max(0, -steps), min(count, count - steps))
    return lax.ppermute(value, axis, [(source, source + steps) for source in range(leading, last)])


def attend(groups, key_rows, value_rows):
    width = key_rows.shape[1]
    heads = width // HD
    scale = HD ** (-0.5)
    query_sets = [(rows_q.reshape(rows_q.shape[0], heads, HD), pos_q) for rows_q, pos_q in groups]

    def update(state, queries, query_pos, keys_here, values_here, key_pos):
        running_top, running_total, running_sum = state
        scores = (
            jnp.einsum("qhd,khd->hqk", queries, keys_here, preferred_element_type=jnp.float32)
            * scale
        )
        allowed = (key_pos[None, :] <= query_pos[:, None])[None]
        masked = jnp.where(allowed, scores, masked_floor)
        new_top = jnp.maximum(running_top, jnp.max(masked, axis=-1))
        weights = jnp.where(allowed, jnp.exp(masked - new_top[..., None]), 0.0)
        rescale = jnp.exp(running_top - new_top)
        new_total = running_total * rescale + jnp.sum(weights, axis=-1)
        new_sum = running_sum * rescale[..., None] + jnp.einsum(
            "hqk,khd->hqd",
            weights.astype(jnp.bfloat16),
            values_here,
            preferred_element_type=jnp.float32,
        )
        return (new_top, new_total, new_sum)

    initial = tuple(
        (
            (
                jnp.full((heads, pos_q.shape[0]), masked_floor, jnp.float32),
                jnp.zeros((heads, pos_q.shape[0]), jnp.float32),
                jnp.zeros((heads, pos_q.shape[0], HD), jnp.float32),
            )
            for rows_q, pos_q in groups
        )
    )
    pieces = (
        lax.all_gather(key_rows, "ctx", axis=0, tiled=True),
        lax.all_gather(value_rows, "ctx", axis=0, tiled=True),
    )
    count = pieces[0].shape[0]
    blocks = count // count
    keys_all = pieces[0].reshape(blocks, count, heads, HD)
    values_all = pieces[1].reshape(blocks, count, heads, HD)
    index_rows = jnp.arange(count)
    pos_all = index_rows.reshape(blocks, count)

    def fold_step(states, block):
        keys_here, values_here, key_pos = block
        return (
            tuple(
                (
                    update(
                        states[g],
                        query_sets[g][0],
                        query_sets[g][1],
                        keys_here,
                        values_here,
                        key_pos,
                    )
                    for g in range(len(query_sets))
                )
            ),
            None,
        )

    result, _ = lax.scan(fold_step, initial, (keys_all, values_all, pos_all))
    return [(final[2] / final[1][..., None]).astype(jnp.bfloat16) for final in result]

def recurrence_states(signal_ref, rates_ref, ends_ref, state_ref):
    rows = signal_ref.shape[0]
    poles = rates_ref.shape[0]
    step = rows // CHUNKS
    decays = [
        jnp.broadcast_to(jnp.exp(-rates_ref[n : n + 1, :]), (CHUNKS, LANES)) for n in range(poles)
    ]

    def advance(i, states):
        piece = signal_ref[pl.ds(i, CHUNKS, stride=step), :]
        return tuple(decay * state + piece for decay, state in zip(decays, states))

    start = tuple(jnp.zeros((CHUNKS, LANES), jnp.float32) for _ in range(poles))
    ends = lax.fori_loop(0, step, advance, start, unroll=4)
    for n in range(poles):
        ends_ref[:, n, :] = ends[n]
    span = jnp.exp(-rates_ref[...] * float(step))
    total = jnp.zeros((poles, LANES), jnp.float32)
    for chunk in range(CHUNKS):
        total = span * total + ends_ref[chunk]
    state_ref[...] = total


def recurrence_outputs(signal_ref, rates_ref, residues_ref, ends_ref, before, conv_ref):
    rows = signal_ref.shape[0]
    poles = rates_ref.shape[0]
    step = rows // CHUNKS
    span = jnp.exp(-rates_ref[...] * float(step))
    for chunk in range(CHUNKS):
        here = ends_ref[chunk]
        ends_ref[chunk] = before
        before = span * before + here
    decays = [
        jnp.broadcast_to(jnp.exp(-rates_ref[n : n + 1, :]), (CHUNKS, LANES)) for n in range(poles)
    ]
    weights = [jnp.broadcast_to(residues_ref[n : n + 1, :], (CHUNKS, LANES)) for n in range(poles)]

    def advance(i, states):
        rows_here = pl.ds(i, CHUNKS, stride=step)
        piece = signal_ref[rows_here, :]
        states = tuple(decay * state + piece for decay, state in zip(decays, states))
        terms = [weight * state for weight, state in zip(weights, states)]
        while len(terms) > 1:
            terms = [sum(terms[i : i + 2][1:], terms[i]) for i in range(0, len(terms), 2)]
        conv_ref[rows_here, :] = terms[0]
        return states

    lax.fori_loop(0, step, advance, tuple(ends_ref[:, n, :] for n in range(poles)), unroll=2)


def make_signal(attended_ref, rim_ref, gate_ref, taps_ref, stream_ref, signal_ref):
    rows = attended_ref.shape[0]
    taps = taps_ref.shape[0]
    pad = rim_ref.shape[0]
    stream_ref[:pad, :] = rim_ref[...].astype(jnp.float32)
    stream_ref[pad:, :] = attended_ref[...].astype(jnp.float32)
    mixed = taps_ref[0:1, :] * stream_ref[pad : pad + rows, :]
    for tap in range(1, taps):
        mixed = mixed + taps_ref[tap : tap + 1, :] * stream_ref[pad - tap : pad - tap + rows, :]
    signal_ref[...] = gate_ref[...].astype(jnp.float32) * mixed


def states_kernel(attended_ref, rim_ref, gate_ref, taps_ref, rates_ref, signal_ref, ends_ref, state_ref, stream_ref):
    make_signal(attended_ref, rim_ref, gate_ref, taps_ref, stream_ref, signal_ref)
    recurrence_states(signal_ref, rates_ref, ends_ref, state_ref)


def outputs_kernel(signal_ref, ends_ref, before_ref, rates_ref, residues_ref, skip_ref, gate_ref, out_ref, held_ref, conv_ref):
    held_ref[...] = ends_ref[...]
    recurrence_outputs(signal_ref, rates_ref, residues_ref, held_ref, before_ref[...], conv_ref)
    mixed = conv_ref[...] + skip_ref[...] * signal_ref[...]
    out_ref[...] = (gate_ref[...].astype(jnp.float32) * mixed).astype(jnp.bfloat16)


def by_lanes(rows):
    return pl.BlockSpec((rows, LANES), lambda g: (0, g))


def hyena(attended, gate_in, gate_out, short_taps, decay_rates, residues, skip_gain):
    rows, width = attended.shape
    taps = short_taps.shape[0]
    poles = decay_rates.shape[0]
    segment = lax.axis_index("ctx")
    groups = width // LANES
    pad = 16
    rim = from_behind(attended[rows - pad :], "ctx", 1)
    ends_spec = pl.BlockSpec((CHUNKS, poles, LANES), lambda g: (0, 0, g))
    signal, ends, state = pl.pallas_call(
        states_kernel,
        grid=(groups,),
        in_specs=[by_lanes(rows), by_lanes(pad), by_lanes(rows), by_lanes(taps), by_lanes(poles)],
        out_specs=[by_lanes(rows), ends_spec, by_lanes(poles)],
        out_shape=[
            jax.ShapeDtypeStruct((rows, width), jnp.float32),
            jax.ShapeDtypeStruct((CHUNKS, poles, width), jnp.float32),
            jax.ShapeDtypeStruct((poles, width), jnp.float32),
        ],
        scratch_shapes=[pltpu.VMEM((pad + rows, LANES), jnp.float32)],
    )(attended, rim, gate_in, short_taps, decay_rates)
    states = lax.all_gather(state, "ctx", axis=0)
    earlier = jnp.arange(states.shape[0])
    gap = jnp.maximum((segment - earlier - 1) * rows, 0).astype(jnp.float32)
    factor = jnp.where(
        (earlier < segment)[:, None, None], jnp.exp(-decay_rates[None] * gap[:, None, None]), 0.0
    )
    before = jnp.sum(factor * states, axis=0)
    return pl.pallas_call(
        outputs_kernel,
        grid=(groups,),
        in_specs=[
            by_lanes(rows), ends_spec, by_lanes(poles), by_lanes(poles), by_lanes(poles), by_lanes(1), by_lanes(rows),
        ],
        out_specs=by_lanes(rows),
        out_shape=jax.ShapeDtypeStruct((rows, width), jnp.bfloat16),
        scratch_shapes=[
            pltpu.VMEM((CHUNKS, poles, LANES), jnp.float32),
            pltpu.VMEM((rows, LANES), jnp.float32),
        ],
    )(signal, ends, before, decay_rates, residues, skip_gain[None], gate_out)


def per_device(
    residual_in,
    query_rows,
    key_rows,
    value_rows,
    out_weight,
    gate_in,
    gate_out,
    short_taps,
    decay_rates,
    residues,
    skip_gain,
):
    rows, width = residual_in.shape
    segments = lax.axis_size("ctx")
    heads = width // HD
    if heads % segments == 0:
        heads_out = spread_attention(query_rows, key_rows, value_rows)
    else:
        query_pos = lax.axis_index("ctx") * rows + jnp.arange(rows)
        heads_out = attend([(query_rows, query_pos)], key_rows, value_rows)[0]
        heads_out = heads_out.transpose(1, 0, 2).reshape(rows, width)
    if lax.axis_size("mp") == 8:
        attended = project_reduce(heads_out, residual_in, out_weight)
    else:
        partial = jnp.einsum(
            "qk,kc->cq", heads_out, out_weight, preferred_element_type=jnp.float32
        ).astype(jnp.bfloat16)
        projected = lax.psum_scatter(partial, "mp", scatter_dimension=0, tiled=True)
        attended = (
            residual_in.astype(jnp.float32) + projected.astype(jnp.float32).T
        ).astype(jnp.bfloat16)
    hyena_out = hyena(attended, gate_in, gate_out, short_taps, decay_rates, residues, skip_gain)
    return (attended, hyena_out)


def solution(mesh):
    in_specs = (
        P("ctx", "mp"),
        P("ctx", "mp"),
        P("ctx", "mp"),
        P("ctx", "mp"),
        P("mp", None),
        P("ctx", "mp"),
        P("ctx", "mp"),
        P(None, "mp"),
        P(None, "mp"),
        P(None, "mp"),
        P("mp"),
    )
    out_specs = (P("ctx", "mp"), P("ctx", "mp"))
    return jax.shard_map(
        per_device, mesh=mesh, in_specs=in_specs, out_specs=out_specs, check_vma=False
    )
```

```python
import functools
import math

import jax
import jax.numpy as jnp
from jax import lax
from jax.experimental import pallas as pl
from jax.experimental.pallas import tpu as pltpu
from jax.sharding import PartitionSpec as P

HD = 128
LANES = 128
CHUNKS = 8
masked_floor = -1e30

MESH = pl.DeviceIdType.MESH


def attend_block(query_ref, key_ref, value_ref, out_ref, start, block):
    factor = HD ** (-0.5) * math.log2(math.e)
    row = lax.broadcasted_iota(jnp.int32, (block, block), 0)
    column = lax.broadcasted_iota(jnp.int32, (block, block), 1)
    contract_last = (((1,), (1,)), ((), ()))
    queries = query_ref[start : start + block, :]
    diagonal = lax.dot_general(
        queries,
        key_ref[start : start + block, :],
        contract_last,
        preferred_element_type=jnp.float32,
    )
    diagonal = jnp.where(column <= row, diagonal, masked_floor)
    highest = jnp.max(diagonal, axis=1, keepdims=True)
    if start:
        earlier = lax.dot_general(
            queries, key_ref[:start, :], contract_last, preferred_element_type=jnp.float32
        )
        highest = jnp.maximum(highest, jnp.max(earlier, axis=1, keepdims=True))
    shift = highest * factor
    weights = jnp.exp2(diagonal * factor - shift)
    total = jnp.sum(weights, axis=1, keepdims=True)
    summed = jnp.dot(
        weights.astype(jnp.bfloat16),
        value_ref[start : start + block, :],
        preferred_element_type=jnp.float32,
    )
    if start:
        weights = jnp.exp2(earlier * factor - shift)
        total = total + jnp.sum(weights, axis=1, keepdims=True)
        summed = summed + jnp.dot(
            weights.astype(jnp.bfloat16), value_ref[:start, :], preferred_element_type=jnp.float32
        )
    out_ref[start : start + block, :] = (summed / total).astype(jnp.bfloat16)


def spread_attention_kernel(
    n, block, query_ref, key_ref, value_ref, out_ref,
    queries, keys, values, results, send, recv, own, back_send, back_recv, back_own,
):
    me = lax.axis_index("ctx")
    rows = query_ref.shape[0]
    heads = queries.shape[0]
    barrier = pltpu.get_barrier_semaphore()
    for p in range(1, n):
        pl.semaphore_signal(
            barrier, inc=1, device_id={"ctx": lax.rem(me + p, n)}, device_id_type=MESH
        )
    pl.semaphore_wait(barrier, n - 1)

    sources = (key_ref, query_ref, value_ref)
    slots = (keys, queries, values)
    my_rows = pl.ds(pl.multiple_of(me * rows, rows), rows)
    arrivals = []
    own_copies = []
    for head in range(heads):
        arrivals.append([])
        own_copies.append([])
        for t in range(3):
            for p in range(n):
                target = lax.rem(me + p, n)
                columns = pl.ds(pl.multiple_of((target * heads + head) * HD, HD), HD)
                source = sources[t].at[:, columns]
                landing = slots[t].at[head, my_rows, :]
                if p == 0:
                    copy = pltpu.make_async_copy(source, landing, own.at[head, t])
                    own_copies[head].append(copy)
                else:
                    copy = pltpu.make_async_remote_copy(
                        src_ref=source,
                        dst_ref=landing,
                        send_sem=send.at[head, t, p],
                        recv_sem=recv.at[head, t, p],
                        device_id={"ctx": target},
                        device_id_type=MESH,
                    )
                    arrivals[head].append(copy)
                copy.start()

    returned = []
    for head in range(heads):
        for copy in own_copies[head]:
            copy.wait()
        for copy in arrivals[head]:
            copy.wait_recv()
        columns = pl.ds(pl.multiple_of((me * heads + head) * HD, HD), HD)
        landing = out_ref.at[:, columns]
        for segment in range(n):
            for start in range(segment * rows, (segment + 1) * rows, block):
                attend_block(
                    queries.at[head], keys.at[head], values.at[head], results.at[head], start, block
                )
            source = results.at[head, pl.ds(segment * rows, rows), :]
            away = lax.rem(segment - me + n, n)

            @pl.when(away != 0)
            def _():
                pltpu.make_async_remote_copy(
                    src_ref=source,
                    dst_ref=landing,
                    send_sem=back_send.at[head, away],
                    recv_sem=back_recv.at[head, away],
                    device_id={"ctx": segment},
                    device_id_type=MESH,
                ).start()

            @pl.when(away == 0)
            def _():
                pltpu.make_async_copy(source, landing, back_own.at[head]).start()

    for head in range(heads):
        source = results.at[head, pl.ds(0, rows), :]
        landing = out_ref.at[:, pl.ds(0, HD)]
        pltpu.make_async_copy(source, landing, back_own.at[head]).wait()
        for p in range(1, n):
            copy = pltpu.make_async_remote_copy(
                src_ref=source,
                dst_ref=landing,
                send_sem=back_send.at[head, p],
                recv_sem=back_recv.at[head, p],
                device_id={"ctx": lax.rem(me + p, n)},
                device_id_type=MESH,
            )
            copy.wait_send()
            copy.wait_recv()
        for copy in arrivals[head]:
            copy.wait_send()


def spread_attention(query_rows, key_rows, value_rows):
    rows, width = query_rows.shape
    n = lax.axis_size("ctx")
    heads = width // HD // n
    length = n * rows
    whole = pltpu.VMEM((heads, length, HD), jnp.bfloat16)
    dma = pltpu.SemaphoreType.DMA
    return pl.pallas_call(
        functools.partial(spread_attention_kernel, n, min(256, rows)),
        in_specs=[pl.BlockSpec(memory_space=pl.ANY)] * 3,
        out_specs=pl.BlockSpec(memory_space=pl.ANY),
        out_shape=jax.ShapeDtypeStruct((rows, width), jnp.bfloat16),
        scratch_shapes=[
            whole, whole, whole, whole,
            dma((heads, 3, n)), dma((heads, 3, n)), dma((heads, 3)),
            dma((heads, n)), dma((heads, n)), dma((heads,)),
        ],
        compiler_params=pltpu.CompilerParams(
            collective_id=1, has_side_effects=True, vmem_limit_bytes=48 * 1024 * 1024
        ),
        cost_estimate=pl.CostEstimate(
            flops=2 * length * length * heads * HD,
            bytes_accessed=8 * rows * width,
            transcendentals=heads * length * length // 2,
        ),
    )(query_rows, key_rows, value_rows)


def project_hyena_kernel(
    n, heads_ref, residual_ref, weight_ref, gate_in_ref, gate_out_ref, taps_ref, rates_ref,
    residues_ref, skip_ref, out_ref, hyena_ref,
    weights, for_pair, from_pair, sums, from_end, from_mid,
    rim, stream, signal, conv, ends, state_out, states_in,
    weight_sem, pair_send, pair_recv, end_send, end_recv, mid_send, mid_recv, back_send,
    rim_send, rim_recv, state_send, state_recv,
):
    mp = lax.axis_index("mp")
    core = lax.rem(mp, 2)
    chip = mp // 2
    mirrored = chip >= 2
    middle = jnp.logical_or(chip == 1, chip == 2)
    step = jnp.where(mirrored, -1, 1)
    pair = chip * 2 + 1 - core
    toward = (chip + step) * 2 + core
    behind = (chip - step) * 2 + core
    segment = lax.axis_index("ctx")
    rows, width = residual_ref.shape
    parts = end_send.shape[1]
    part = width // parts
    poles = rates_ref.shape[0]
    pad = rim.shape[0]

    for p in range(1, n):

        @pl.when(segment < p)
        def _():
            states_in[p] = jnp.zeros(states_in.shape[1:], jnp.float32)

    @pl.when(segment == 0)
    def _():
        rim[...] = jnp.zeros(rim.shape, rim.dtype)

    copies = {}
    for h in range(parts):
        for mine in range(2):
            for k in range(4):
                target = jnp.where(mirrored, k, 3 - k)
                owner = target * 2 + (core if mine else 1 - core)
                columns = pl.ds(pl.multiple_of(owner * width + h * part, part), part)
                copies[h, k, mine] = pltpu.make_async_copy(
                    weight_ref.at[:, columns],
                    weights.at[k, mine, :, pl.ds(h * part, part)],
                    weight_sem.at[h, k, mine],
                )
                copies[h, k, mine].start()

    barrier = pltpu.get_barrier_semaphore()
    for p in range(1, n):
        pl.semaphore_signal(
            barrier, inc=1, device_id={"ctx": lax.rem(segment + p, n)}, device_id_type=MESH
        )
    pl.semaphore_signal(barrier, inc=1, device_id={"mp": pair}, device_id_type=MESH)
    pl.semaphore_signal(barrier, inc=1, device_id={"mp": toward}, device_id_type=MESH)

    @pl.when(middle)
    def _():
        pl.semaphore_signal(barrier, inc=1, device_id={"mp": behind}, device_id_type=MESH)
        pl.semaphore_wait(barrier, 3 + n - 1)

    @pl.when(jnp.logical_not(middle))
    def _():
        pl.semaphore_wait(barrier, 2 + n - 1)

    def cut(h):
        return pl.ds(h * part, part)

    def part_copy(source, landing, slot, h, send_sem, recv_sem, device):
        return pltpu.make_async_remote_copy(
            src_ref=source.at[slot[0], :, cut(h)],
            dst_ref=landing.at[slot[1], :, cut(h)],
            send_sem=send_sem,
            recv_sem=recv_sem,
            device_id={"mp": device},
            device_id_type=MESH,
        )

    def to_pair(k, h):
        return part_copy(
            for_pair, from_pair, (k, k), h, pair_send.at[k, h], pair_recv.at[k, h], pair
        )

    def to_middle(k, h):
        return part_copy(sums, from_end, (k, k), h, end_send.at[k, h], end_recv.at[k, h], toward)

    def across(k, h):
        return part_copy(sums, from_mid, (k, k), h, mid_send.at[k, h], mid_recv.at[k, h], toward)

    def to_end(h):
        return part_copy(sums, from_mid, (3, 0), h, back_send.at[h], mid_recv.at[0, h], behind)

    for h in range(parts):
        for k in range(4):
            copies[h, k, 0].wait()
            for_pair[k, :, cut(h)] = jnp.dot(
                heads_ref[...], weights[k, 0, :, cut(h)], preferred_element_type=jnp.float32
            ).astype(jnp.bfloat16)
            to_pair(k, h).start()
        for k in range(4):
            copies[h, k, 1].wait()
            mixed = jnp.dot(
                heads_ref[...], weights[k, 1, :, cut(h)], preferred_element_type=jnp.float32
            )
            to_pair(k, h).wait_recv()
            sums[k, :, cut(h)] = (mixed + from_pair[k, :, cut(h)].astype(jnp.float32)).astype(
                jnp.bfloat16
            )
            if k < 3:

                @pl.when(jnp.logical_not(middle))
                def _():
                    to_middle(k, h).start()

    def add(k, h, landing, slot):
        total = sums[k, :, cut(h)].astype(jnp.float32) + landing[slot, :, cut(h)].astype(jnp.float32)
        sums[k, :, cut(h)] = total.astype(jnp.bfloat16)

    def finish(h, k, landings):
        total = sums[k, :, cut(h)].astype(jnp.float32)
        for landing, slot in landings:
            total = total + landing[slot, :, cut(h)].astype(jnp.float32)
        out_ref[:, cut(h)] = (residual_ref[:, cut(h)].astype(jnp.float32) + total).astype(
            jnp.bfloat16
        )

    def rim_copy(h):
        return pltpu.make_async_remote_copy(
            src_ref=out_ref.at[pl.ds(rows - pad, pad), cut(h)],
            dst_ref=rim.at[:, cut(h)],
            send_sem=rim_send.at[h],
            recv_sem=rim_recv.at[h],
            device_id={"ctx": lax.rem(segment + 1, n)},
            device_id_type=MESH,
        )

    def state_copy(p, h):
        return pltpu.make_async_remote_copy(
            src_ref=state_out.at[:, cut(h)],
            dst_ref=states_in.at[p, :, cut(h)],
            send_sem=state_send.at[p, h],
            recv_sem=state_recv.at[p, h],
            device_id={"ctx": lax.rem(segment + p, n)},
            device_id_type=MESH,
        )

    def groups_of(h):
        return pl.loop(h * part // LANES, (h + 1) * part // LANES)

    def lanes_of(g):
        return pl.ds(pl.multiple_of(g * LANES, LANES), LANES)

    def states_part(h):
        @pl.when(segment > 0)
        def _():
            rim_copy(h).wait_recv()

        @groups_of(h)
        def _(g):
            lanes = lanes_of(g)
            make_signal(
                out_ref.at[:, lanes], rim.at[:, lanes], gate_in_ref.at[:, lanes],
                taps_ref.at[:, lanes], stream, signal.at[g],
            )
            recurrence_states(signal.at[g], rates_ref.at[:, lanes], ends.at[g], state_out.at[:, lanes])

        for p in range(1, n):

            @pl.when(segment + p < n)
            def _():
                state_copy(p, h).start()

    def outputs_part(h):
        for p in range(1, n):

            @pl.when(segment >= p)
            def _():
                state_copy(p, h).wait_recv()

        @groups_of(h)
        def _(g):
            lanes = lanes_of(g)
            rates = rates_ref.at[:, lanes]
            span = jnp.exp(-rates[...] * float(rows))
            before = jnp.zeros((poles, LANES), jnp.float32)
            for p in range(n - 1, 0, -1):
                before = span * before + states_in[p, :, lanes]
            recurrence_outputs(signal.at[g], rates, residues_ref.at[:, lanes], ends.at[g], before, conv)
            mixed = conv[...] + skip_ref[:, lanes] * signal[g]
            hyena_ref[:, lanes] = (gate_out_ref[:, lanes].astype(jnp.float32) * mixed).astype(
                jnp.bfloat16
            )

    for h in range(parts):

        @pl.when(middle)
        def _():
            for k in range(2):
                to_middle(k, h).wait_recv()
                add(k, h, from_end, k)
                across(k, h).start()
            across(0, h).wait_recv()
            add(3, h, from_mid, 0)
            to_end(h).start()
            to_middle(2, h).wait_recv()
            across(1, h).wait_recv()
            finish(h, 2, ((from_end, 2), (from_mid, 1)))

        @pl.when(jnp.logical_not(middle))
        def _():
            across(0, h).wait_recv()
            finish(h, 3, ((from_mid, 0),))

        @pl.when(segment < n - 1)
        def _():
            rim_copy(h).start()

        if h:
            outputs_part(h - 1)
        states_part(h)
    outputs_part(parts - 1)

    for h in range(parts):
        for k in range(4):
            to_pair(k, h).wait_send()

        @pl.when(middle)
        def _():
            across(0, h).wait_send()
            across(1, h).wait_send()
            to_end(h).wait_send()

        @pl.when(jnp.logical_not(middle))
        def _():
            for k in range(3):
                to_middle(k, h).wait_send()

        @pl.when(segment < n - 1)
        def _():
            rim_copy(h).wait_send()

        for p in range(1, n):

            @pl.when(segment + p < n)
            def _():
                state_copy(p, h).wait_send()


def project_hyena(
    heads_out, residual_in, out_weight, gate_in, gate_out, short_taps, decay_rates, residues, skip_gain
):
    rows, width = residual_in.shape
    depth = heads_out.shape[1]
    n = lax.axis_size("ctx")
    poles = decay_rates.shape[0]
    groups = width // LANES
    parts = min(4, groups)
    pad = 16
    vmem = pl.BlockSpec(memory_space=pltpu.VMEM)
    dma = pltpu.SemaphoreType.DMA
    block = jax.ShapeDtypeStruct((rows, width), jnp.bfloat16)

    def blocks(count):
        return pltpu.VMEM((count, rows, width), jnp.bfloat16)

    def floats(*dims):
        return pltpu.VMEM(dims, jnp.float32)

    return pl.pallas_call(
        functools.partial(project_hyena_kernel, n),
        in_specs=[vmem, vmem, pl.BlockSpec(memory_space=pl.ANY)] + [vmem] * 6,
        out_specs=[vmem, vmem],
        out_shape=[block, block],
        scratch_shapes=[
            pltpu.VMEM((4, 2, depth, width), jnp.bfloat16),
            blocks(4), blocks(4), blocks(4), blocks(3), blocks(2),
            pltpu.VMEM((pad, width), jnp.bfloat16),
            floats(pad + rows, LANES), floats(groups, rows, LANES), floats(rows, LANES),
            floats(groups, CHUNKS, poles, LANES), floats(poles, width), floats(n, poles, width),
            dma((parts, 4, 2)), dma((4, parts)), dma((4, parts)),
            dma((3, parts)), dma((3, parts)), dma((2, parts)), dma((2, parts)), dma((parts,)),
            dma((parts,)), dma((parts,)), dma((n, parts)), dma((n, parts)),
        ],
        compiler_params=pltpu.CompilerParams(
            collective_id=2, has_side_effects=True, vmem_limit_bytes=58 * 1024 * 1024
        ),
        cost_estimate=pl.CostEstimate(
            flops=16 * rows * depth * width,
            bytes_accessed=16 * depth * width + 12 * rows * width,
            transcendentals=0,
        ),
    )(
        heads_out, residual_in, out_weight, gate_in, gate_out, short_taps, decay_rates, residues,
        skip_gain[None],
    )


def from_behind(value, axis, steps):
    count = lax.axis_size(axis)
    leading, last = (max(0, -steps), min(count, count - steps))
    return lax.ppermute(value, axis, [(source, source + steps) for source in range(leading, last)])


def attend(groups, key_rows, value_rows):
    width = key_rows.shape[1]
    heads = width // HD
    scale = HD ** (-0.5)
    query_sets = [(rows_q.reshape(rows_q.shape[0], heads, HD), pos_q) for rows_q, pos_q in groups]

    def update(state, queries, query_pos, keys_here, values_here, key_pos):
        running_top, running_total, running_sum = state
        scores = (
            jnp.einsum("qhd,khd->hqk", queries, keys_here, preferred_element_type=jnp.float32)
            * scale
        )
        allowed = (key_pos[None, :] <= query_pos[:, None])[None]
        masked = jnp.where(allowed, scores, masked_floor)
        new_top = jnp.maximum(running_top, jnp.max(masked, axis=-1))
        weights = jnp.where(allowed, jnp.exp(masked - new_top[..., None]), 0.0)
        rescale = jnp.exp(running_top - new_top)
        new_total = running_total * rescale + jnp.sum(weights, axis=-1)
        new_sum = running_sum * rescale[..., None] + jnp.einsum(
            "hqk,khd->hqd",
            weights.astype(jnp.bfloat16),
            values_here,
            preferred_element_type=jnp.float32,
        )
        return (new_top, new_total, new_sum)

    initial = tuple(
        (
            (
                jnp.full((heads, pos_q.shape[0]), masked_floor, jnp.float32),
                jnp.zeros((heads, pos_q.shape[0]), jnp.float32),
                jnp.zeros((heads, pos_q.shape[0], HD), jnp.float32),
            )
            for rows_q, pos_q in groups
        )
    )
    pieces = (
        lax.all_gather(key_rows, "ctx", axis=0, tiled=True),
        lax.all_gather(value_rows, "ctx", axis=0, tiled=True),
    )
    count = pieces[0].shape[0]
    blocks = count // count
    keys_all = pieces[0].reshape(blocks, count, heads, HD)
    values_all = pieces[1].reshape(blocks, count, heads, HD)
    index_rows = jnp.arange(count)
    pos_all = index_rows.reshape(blocks, count)

    def fold_step(states, block):
        keys_here, values_here, key_pos = block
        return (
            tuple(
                (
                    update(
                        states[g],
                        query_sets[g][0],
                        query_sets[g][1],
                        keys_here,
                        values_here,
                        key_pos,
                    )
                    for g in range(len(query_sets))
                )
            ),
            None,
        )

    result, _ = lax.scan(fold_step, initial, (keys_all, values_all, pos_all))
    return [(final[2] / final[1][..., None]).astype(jnp.bfloat16) for final in result]

def recurrence_states(signal_ref, rates_ref, ends_ref, state_ref):
    rows = signal_ref.shape[0]
    poles = rates_ref.shape[0]
    step = rows // CHUNKS
    decays = [
        jnp.broadcast_to(jnp.exp(-rates_ref[n : n + 1, :]), (CHUNKS, LANES)) for n in range(poles)
    ]

    def advance(i, states):
        piece = signal_ref[pl.ds(i, CHUNKS, stride=step), :]
        return tuple(decay * state + piece for decay, state in zip(decays, states))

    start = tuple(jnp.zeros((CHUNKS, LANES), jnp.float32) for _ in range(poles))
    ends = lax.fori_loop(0, step, advance, start, unroll=4)
    for n in range(poles):
        ends_ref[:, n, :] = ends[n]
    span = jnp.exp(-rates_ref[...] * float(step))
    total = jnp.zeros((poles, LANES), jnp.float32)
    for chunk in range(CHUNKS):
        total = span * total + ends_ref[chunk]
    state_ref[...] = total


def recurrence_outputs(signal_ref, rates_ref, residues_ref, ends_ref, before, conv_ref):
    rows = signal_ref.shape[0]
    poles = rates_ref.shape[0]
    step = rows // CHUNKS
    span = jnp.exp(-rates_ref[...] * float(step))
    for chunk in range(CHUNKS):
        here = ends_ref[chunk]
        ends_ref[chunk] = before
        before = span * before + here
    decays = [
        jnp.broadcast_to(jnp.exp(-rates_ref[n : n + 1, :]), (CHUNKS, LANES)) for n in range(poles)
    ]
    weights = [jnp.broadcast_to(residues_ref[n : n + 1, :], (CHUNKS, LANES)) for n in range(poles)]

    def advance(i, states):
        rows_here = pl.ds(i, CHUNKS, stride=step)
        piece = signal_ref[rows_here, :]
        states = tuple(decay * state + piece for decay, state in zip(decays, states))
        terms = [weight * state for weight, state in zip(weights, states)]
        while len(terms) > 1:
            terms = [sum(terms[i : i + 2][1:], terms[i]) for i in range(0, len(terms), 2)]
        conv_ref[rows_here, :] = terms[0]
        return states

    lax.fori_loop(0, step, advance, tuple(ends_ref[:, n, :] for n in range(poles)), unroll=2)


def make_signal(attended_ref, rim_ref, gate_ref, taps_ref, stream_ref, signal_ref):
    rows = attended_ref.shape[0]
    taps = taps_ref.shape[0]
    pad = rim_ref.shape[0]
    stream_ref[:pad, :] = rim_ref[...].astype(jnp.float32)
    stream_ref[pad:, :] = attended_ref[...].astype(jnp.float32)
    mixed = taps_ref[0:1, :] * stream_ref[pad : pad + rows, :]
    for tap in range(1, taps):
        mixed = mixed + taps_ref[tap : tap + 1, :] * stream_ref[pad - tap : pad - tap + rows, :]
    signal_ref[...] = gate_ref[...].astype(jnp.float32) * mixed


def states_kernel(attended_ref, rim_ref, gate_ref, taps_ref, rates_ref, signal_ref, ends_ref, state_ref, stream_ref):
    make_signal(attended_ref, rim_ref, gate_ref, taps_ref, stream_ref, signal_ref)
    recurrence_states(signal_ref, rates_ref, ends_ref, state_ref)


def outputs_kernel(signal_ref, ends_ref, before_ref, rates_ref, residues_ref, skip_ref, gate_ref, out_ref, held_ref, conv_ref):
    held_ref[...] = ends_ref[...]
    recurrence_outputs(signal_ref, rates_ref, residues_ref, held_ref, before_ref[...], conv_ref)
    mixed = conv_ref[...] + skip_ref[...] * signal_ref[...]
    out_ref[...] = (gate_ref[...].astype(jnp.float32) * mixed).astype(jnp.bfloat16)


def by_lanes(rows):
    return pl.BlockSpec((rows, LANES), lambda g: (0, g))


def hyena(attended, gate_in, gate_out, short_taps, decay_rates, residues, skip_gain):
    rows, width = attended.shape
    taps = short_taps.shape[0]
    poles = decay_rates.shape[0]
    segment = lax.axis_index("ctx")
    groups = width // LANES
    pad = 16
    rim = from_behind(attended[rows - pad :], "ctx", 1)
    ends_spec = pl.BlockSpec((CHUNKS, poles, LANES), lambda g: (0, 0, g))
    signal, ends, state = pl.pallas_call(
        states_kernel,
        grid=(groups,),
        in_specs=[by_lanes(rows), by_lanes(pad), by_lanes(rows), by_lanes(taps), by_lanes(poles)],
        out_specs=[by_lanes(rows), ends_spec, by_lanes(poles)],
        out_shape=[
            jax.ShapeDtypeStruct((rows, width), jnp.float32),
            jax.ShapeDtypeStruct((CHUNKS, poles, width), jnp.float32),
            jax.ShapeDtypeStruct((poles, width), jnp.float32),
        ],
        scratch_shapes=[pltpu.VMEM((pad + rows, LANES), jnp.float32)],
    )(attended, rim, gate_in, short_taps, decay_rates)
    states = lax.all_gather(state, "ctx", axis=0)
    earlier = jnp.arange(states.shape[0])
    gap = jnp.maximum((segment - earlier - 1) * rows, 0).astype(jnp.float32)
    factor = jnp.where(
        (earlier < segment)[:, None, None], jnp.exp(-decay_rates[None] * gap[:, None, None]), 0.0
    )
    before = jnp.sum(factor * states, axis=0)
    return pl.pallas_call(
        outputs_kernel,
        grid=(groups,),
        in_specs=[
            by_lanes(rows), ends_spec, by_lanes(poles), by_lanes(poles), by_lanes(poles), by_lanes(1), by_lanes(rows),
        ],
        out_specs=by_lanes(rows),
        out_shape=jax.ShapeDtypeStruct((rows, width), jnp.bfloat16),
        scratch_shapes=[
            pltpu.VMEM((CHUNKS, poles, LANES), jnp.float32),
            pltpu.VMEM((rows, LANES), jnp.float32),
        ],
    )(signal, ends, before, decay_rates, residues, skip_gain[None], gate_out)


def per_device(
    residual_in,
    query_rows,
    key_rows,
    value_rows,
    out_weight,
    gate_in,
    gate_out,
    short_taps,
    decay_rates,
    residues,
    skip_gain,
):
    rows, width = residual_in.shape
    segments = lax.axis_size("ctx")
    heads = width // HD
    if heads % segments == 0:
        heads_out = spread_attention(query_rows, key_rows, value_rows)
    else:
        query_pos = lax.axis_index("ctx") * rows + jnp.arange(rows)
        heads_out = attend([(query_rows, query_pos)], key_rows, value_rows)[0]
        heads_out = heads_out.transpose(1, 0, 2).reshape(rows, width)
    if lax.axis_size("mp") == 8:
        return tuple(
            project_hyena(
                heads_out, residual_in, out_weight, gate_in, gate_out, short_taps, decay_rates,
                residues, skip_gain,
            )
        )
    partial = jnp.einsum(
        "qk,kc->cq", heads_out, out_weight, preferred_element_type=jnp.float32
    ).astype(jnp.bfloat16)
    projected = lax.psum_scatter(partial, "mp", scatter_dimension=0, tiled=True)
    attended = (
        residual_in.astype(jnp.float32) + projected.astype(jnp.float32).T
    ).astype(jnp.bfloat16)
    hyena_out = hyena(attended, gate_in, gate_out, short_taps, decay_rates, residues, skip_gain)
    return (attended, hyena_out)


def solution(mesh):
    in_specs = (
        P("ctx", "mp"),
        P("ctx", "mp"),
        P("ctx", "mp"),
        P("ctx", "mp"),
        P("mp", None),
        P("ctx", "mp"),
        P("ctx", "mp"),
        P(None, "mp"),
        P(None, "mp"),
        P(None, "mp"),
        P("mp"),
    )
    out_specs = (P("ctx", "mp"), P("ctx", "mp"))
    return jax.shard_map(
        per_device, mesh=mesh, in_specs=in_specs, out_specs=out_specs, check_vma=False
    )
```

```python
import functools
import math

import jax
import jax.numpy as jnp
from jax import lax
from jax.experimental import pallas as pl
from jax.experimental.pallas import tpu as pltpu
from jax.sharding import PartitionSpec as P

HD = 128
LANES = 128
CHUNKS = 8
masked_floor = -1e30

MESH = pl.DeviceIdType.MESH


def attend_block(query_ref, key_ref, value_ref, out_ref, start, block):
    factor = HD ** (-0.5) * math.log2(math.e)
    row = lax.broadcasted_iota(jnp.int32, (block, block), 0)
    column = lax.broadcasted_iota(jnp.int32, (block, block), 1)
    contract_last = (((1,), (1,)), ((), ()))
    queries = query_ref[start : start + block, :]
    diagonal = lax.dot_general(
        queries,
        key_ref[start : start + block, :],
        contract_last,
        preferred_element_type=jnp.float32,
    )
    diagonal = jnp.where(column <= row, diagonal, masked_floor)
    highest = jnp.max(diagonal, axis=1, keepdims=True)
    if start:
        earlier = lax.dot_general(
            queries, key_ref[:start, :], contract_last, preferred_element_type=jnp.float32
        )
        highest = jnp.maximum(highest, jnp.max(earlier, axis=1, keepdims=True))
    shift = highest * factor
    weights = jnp.exp2(diagonal * factor - shift)
    total = jnp.sum(weights, axis=1, keepdims=True)
    summed = jnp.dot(
        weights.astype(jnp.bfloat16),
        value_ref[start : start + block, :],
        preferred_element_type=jnp.float32,
    )
    if start:
        weights = jnp.exp2(earlier * factor - shift)
        total = total + jnp.sum(weights, axis=1, keepdims=True)
        summed = summed + jnp.dot(
            weights.astype(jnp.bfloat16), value_ref[:start, :], preferred_element_type=jnp.float32
        )
    out_ref[start : start + block, :] = (summed / total).astype(jnp.bfloat16)


def spread_attention_kernel(
    n, block, query_ref, key_ref, value_ref, out_ref,
    queries, keys, values, results, send, recv, own, back_send, back_recv, back_own,
):
    me = lax.axis_index("ctx")
    rows = query_ref.shape[0]
    heads = queries.shape[0]
    barrier = pltpu.get_barrier_semaphore()
    for p in range(1, n):
        pl.semaphore_signal(
            barrier, inc=1, device_id={"ctx": lax.rem(me + p, n)}, device_id_type=MESH
        )
    pl.semaphore_wait(barrier, n - 1)

    sources = (key_ref, query_ref, value_ref)
    slots = (keys, queries, values)
    my_rows = pl.ds(pl.multiple_of(me * rows, rows), rows)
    arrivals = []
    own_copies = []
    for head in range(heads):
        arrivals.append([])
        own_copies.append([])
        for t in range(3):
            for p in range(n):
                target = lax.rem(me + p, n)
                columns = pl.ds(pl.multiple_of((target * heads + head) * HD, HD), HD)
                source = sources[t].at[:, columns]
                landing = slots[t].at[head, my_rows, :]
                if p == 0:
                    copy = pltpu.make_async_copy(source, landing, own.at[head, t])
                    own_copies[head].append(copy)
                else:
                    copy = pltpu.make_async_remote_copy(
                        src_ref=source,
                        dst_ref=landing,
                        send_sem=send.at[head, t, p],
                        recv_sem=recv.at[head, t, p],
                        device_id={"ctx": target},
                        device_id_type=MESH,
                    )
                    arrivals[head].append(copy)
                copy.start()

    returned = []
    for head in range(heads):
        for copy in own_copies[head]:
            copy.wait()
        for copy in arrivals[head]:
            copy.wait_recv()
        columns = pl.ds(pl.multiple_of((me * heads + head) * HD, HD), HD)
        landing = out_ref.at[:, columns]
        for segment in range(n):
            for start in range(segment * rows, (segment + 1) * rows, block):
                attend_block(
                    queries.at[head], keys.at[head], values.at[head], results.at[head], start, block
                )
            source = results.at[head, pl.ds(segment * rows, rows), :]
            away = lax.rem(segment - me + n, n)

            @pl.when(away != 0)
            def _():
                pltpu.make_async_remote_copy(
                    src_ref=source,
                    dst_ref=landing,
                    send_sem=back_send.at[head, away],
                    recv_sem=back_recv.at[head, away],
                    device_id={"ctx": segment},
                    device_id_type=MESH,
                ).start()

            @pl.when(away == 0)
            def _():
                pltpu.make_async_copy(source, landing, back_own.at[head]).start()

    for head in range(heads):
        source = results.at[head, pl.ds(0, rows), :]
        landing = out_ref.at[:, pl.ds(0, HD)]
        pltpu.make_async_copy(source, landing, back_own.at[head]).wait()
        for p in range(1, n):
            copy = pltpu.make_async_remote_copy(
                src_ref=source,
                dst_ref=landing,
                send_sem=back_send.at[head, p],
                recv_sem=back_recv.at[head, p],
                device_id={"ctx": lax.rem(me + p, n)},
                device_id_type=MESH,
            )
            copy.wait_send()
            copy.wait_recv()
        for copy in arrivals[head]:
            copy.wait_send()


def spread_attention(query_rows, key_rows, value_rows):
    rows, width = query_rows.shape
    n = lax.axis_size("ctx")
    heads = width // HD // n
    length = n * rows
    whole = pltpu.VMEM((heads, length, HD), jnp.bfloat16)
    dma = pltpu.SemaphoreType.DMA
    return pl.pallas_call(
        functools.partial(spread_attention_kernel, n, min(256, rows)),
        in_specs=[pl.BlockSpec(memory_space=pl.ANY)] * 3,
        out_specs=pl.BlockSpec(memory_space=pl.ANY),
        out_shape=jax.ShapeDtypeStruct((rows, width), jnp.bfloat16),
        scratch_shapes=[
            whole, whole, whole, whole,
            dma((heads, 3, n)), dma((heads, 3, n)), dma((heads, 3)),
            dma((heads, n)), dma((heads, n)), dma((heads,)),
        ],
        compiler_params=pltpu.CompilerParams(
            collective_id=1, has_side_effects=True, vmem_limit_bytes=60 * 1024 * 1024
        ),
        cost_estimate=pl.CostEstimate(
            flops=2 * length * length * heads * HD,
            bytes_accessed=8 * rows * width,
            transcendentals=heads * length * length // 2,
        ),
    )(query_rows, key_rows, value_rows)


def project_hyena_kernel(
    n, heads_ref, residual_ref, weight_ref, gate_in_ref, gate_out_ref, taps_ref, rates_ref,
    residues_ref, skip_ref, out_ref, hyena_ref,
    weights, for_pair, from_pair, sums, from_end, from_mid,
    rim, stream, signal, conv, ends, state_out, states_in,
    weight_sem, pair_send, pair_recv, end_send, end_recv, mid_send, mid_recv, back_send,
    rim_send, rim_recv, state_send, state_recv,
):
    mp = lax.axis_index("mp")
    core = lax.rem(mp, 2)
    chip = mp // 2
    mirrored = chip >= 2
    middle = jnp.logical_or(chip == 1, chip == 2)
    step = jnp.where(mirrored, -1, 1)
    pair = chip * 2 + 1 - core
    toward = (chip + step) * 2 + core
    behind = (chip - step) * 2 + core
    segment = lax.axis_index("ctx")
    rows, width = residual_ref.shape
    parts = end_send.shape[1]
    part = width // parts
    poles = rates_ref.shape[0]
    pad = rim.shape[0]

    for p in range(1, n):

        @pl.when(segment < p)
        def _():
            states_in[p] = jnp.zeros(states_in.shape[1:], jnp.float32)

    @pl.when(segment == 0)
    def _():
        rim[...] = jnp.zeros(rim.shape, rim.dtype)

    copies = {}
    for h in range(parts):
        for mine in range(2):
            for k in range(4):
                target = jnp.where(mirrored, k, 3 - k)
                owner = target * 2 + (core if mine else 1 - core)
                columns = pl.ds(pl.multiple_of(owner * width + h * part, part), part)
                copies[h, k, mine] = pltpu.make_async_copy(
                    weight_ref.at[:, columns],
                    weights.at[k, mine, :, pl.ds(h * part, part)],
                    weight_sem.at[h, k, mine],
                )
                copies[h, k, mine].start()

    barrier = pltpu.get_barrier_semaphore()
    for p in range(1, n):
        pl.semaphore_signal(
            barrier, inc=1, device_id={"ctx": lax.rem(segment + p, n)}, device_id_type=MESH
        )
    pl.semaphore_signal(barrier, inc=1, device_id={"mp": pair}, device_id_type=MESH)
    pl.semaphore_signal(barrier, inc=1, device_id={"mp": toward}, device_id_type=MESH)

    @pl.when(middle)
    def _():
        pl.semaphore_signal(barrier, inc=1, device_id={"mp": behind}, device_id_type=MESH)
        pl.semaphore_wait(barrier, 3 + n - 1)

    @pl.when(jnp.logical_not(middle))
    def _():
        pl.semaphore_wait(barrier, 2 + n - 1)

    def cut(h):
        return pl.ds(h * part, part)

    def part_copy(source, landing, slot, h, send_sem, recv_sem, device):
        return pltpu.make_async_remote_copy(
            src_ref=source.at[slot[0], :, cut(h)],
            dst_ref=landing.at[slot[1], :, cut(h)],
            send_sem=send_sem,
            recv_sem=recv_sem,
            device_id={"mp": device},
            device_id_type=MESH,
        )

    def to_pair(k, h):
        return part_copy(
            for_pair, from_pair, (k, k), h, pair_send.at[k, h], pair_recv.at[k, h], pair
        )

    def to_middle(k, h):
        return part_copy(sums, from_end, (k, k), h, end_send.at[k, h], end_recv.at[k, h], toward)

    def across(k, h):
        return part_copy(sums, from_mid, (k, k), h, mid_send.at[k, h], mid_recv.at[k, h], toward)

    def to_end(h):
        return part_copy(sums, from_mid, (3, 0), h, back_send.at[h], mid_recv.at[0, h], behind)

    for h in range(parts):
        for k in range(4):
            copies[h, k, 0].wait()
            for_pair[k, :, cut(h)] = jnp.dot(
                heads_ref[...], weights[k, 0, :, cut(h)], preferred_element_type=jnp.float32
            ).astype(jnp.bfloat16)
            to_pair(k, h).start()
        for k in range(4):
            copies[h, k, 1].wait()
            mixed = jnp.dot(
                heads_ref[...], weights[k, 1, :, cut(h)], preferred_element_type=jnp.float32
            )
            to_pair(k, h).wait_recv()
            sums[k, :, cut(h)] = (mixed + from_pair[k, :, cut(h)].astype(jnp.float32)).astype(
                jnp.bfloat16
            )
            if k < 3:

                @pl.when(jnp.logical_not(middle))
                def _():
                    to_middle(k, h).start()

    def add(k, h, landing, slot):
        total = sums[k, :, cut(h)].astype(jnp.float32) + landing[slot, :, cut(h)].astype(jnp.float32)
        sums[k, :, cut(h)] = total.astype(jnp.bfloat16)

    def finish(h, k, landings):
        total = sums[k, :, cut(h)].astype(jnp.float32)
        for landing, slot in landings:
            total = total + landing[slot, :, cut(h)].astype(jnp.float32)
        out_ref[:, cut(h)] = (residual_ref[:, cut(h)].astype(jnp.float32) + total).astype(
            jnp.bfloat16
        )

    def rim_copy(h):
        return pltpu.make_async_remote_copy(
            src_ref=out_ref.at[pl.ds(rows - pad, pad), cut(h)],
            dst_ref=rim.at[:, cut(h)],
            send_sem=rim_send.at[h],
            recv_sem=rim_recv.at[h],
            device_id={"ctx": lax.rem(segment + 1, n)},
            device_id_type=MESH,
        )

    def state_copy(p, h):
        return pltpu.make_async_remote_copy(
            src_ref=state_out.at[:, cut(h)],
            dst_ref=states_in.at[p, :, cut(h)],
            send_sem=state_send.at[p, h],
            recv_sem=state_recv.at[p, h],
            device_id={"ctx": lax.rem(segment + p, n)},
            device_id_type=MESH,
        )

    def groups_of(h):
        return pl.loop(h * part // LANES, (h + 1) * part // LANES)

    def lanes_of(g):
        return pl.ds(pl.multiple_of(g * LANES, LANES), LANES)

    def states_part(h):
        @pl.when(segment > 0)
        def _():
            rim_copy(h).wait_recv()

        @groups_of(h)
        def _(g):
            lanes = lanes_of(g)
            make_signal(
                out_ref.at[:, lanes], rim.at[:, lanes], gate_in_ref.at[:, lanes],
                taps_ref.at[:, lanes], stream, signal.at[g],
            )
            recurrence_states(signal.at[g], rates_ref.at[:, lanes], ends.at[g], state_out.at[:, lanes])

        for p in range(1, n):

            @pl.when(segment + p < n)
            def _():
                state_copy(p, h).start()

    def outputs_part(h):
        for p in range(1, n):

            @pl.when(segment >= p)
            def _():
                state_copy(p, h).wait_recv()

        @groups_of(h)
        def _(g):
            lanes = lanes_of(g)
            rates = rates_ref.at[:, lanes]
            span = jnp.exp(-rates[...] * float(rows))
            before = jnp.zeros((poles, LANES), jnp.float32)
            for p in range(n - 1, 0, -1):
                before = span * before + states_in[p, :, lanes]
            recurrence_outputs(signal.at[g], rates, residues_ref.at[:, lanes], ends.at[g], before, conv)
            mixed = conv[...] + skip_ref[:, lanes] * signal[g]
            hyena_ref[:, lanes] = (gate_out_ref[:, lanes].astype(jnp.float32) * mixed).astype(
                jnp.bfloat16
            )

    for h in range(parts):

        @pl.when(middle)
        def _():
            for k in range(2):
                to_middle(k, h).wait_recv()
                add(k, h, from_end, k)
                across(k, h).start()
            across(0, h).wait_recv()
            add(3, h, from_mid, 0)
            to_end(h).start()
            to_middle(2, h).wait_recv()
            across(1, h).wait_recv()
            finish(h, 2, ((from_end, 2), (from_mid, 1)))

        @pl.when(jnp.logical_not(middle))
        def _():
            across(0, h).wait_recv()
            finish(h, 3, ((from_mid, 0),))

        @pl.when(segment < n - 1)
        def _():
            rim_copy(h).start()

        if h:
            outputs_part(h - 1)
        states_part(h)
    outputs_part(parts - 1)

    for h in range(parts):
        for k in range(4):
            to_pair(k, h).wait_send()

        @pl.when(middle)
        def _():
            across(0, h).wait_send()
            across(1, h).wait_send()
            to_end(h).wait_send()

        @pl.when(jnp.logical_not(middle))
        def _():
            for k in range(3):
                to_middle(k, h).wait_send()

        @pl.when(segment < n - 1)
        def _():
            rim_copy(h).wait_send()

        for p in range(1, n):

            @pl.when(segment + p < n)
            def _():
                state_copy(p, h).wait_send()


def project_hyena(
    heads_out, residual_in, out_weight, gate_in, gate_out, short_taps, decay_rates, residues, skip_gain
):
    rows, width = residual_in.shape
    depth = heads_out.shape[1]
    n = lax.axis_size("ctx")
    poles = decay_rates.shape[0]
    groups = width // LANES
    parts = min(4, groups)
    pad = 16
    vmem = pl.BlockSpec(memory_space=pltpu.VMEM)
    dma = pltpu.SemaphoreType.DMA
    block = jax.ShapeDtypeStruct((rows, width), jnp.bfloat16)

    def blocks(count):
        return pltpu.VMEM((count, rows, width), jnp.bfloat16)

    def floats(*dims):
        return pltpu.VMEM(dims, jnp.float32)

    return pl.pallas_call(
        functools.partial(project_hyena_kernel, n),
        in_specs=[vmem, vmem, pl.BlockSpec(memory_space=pl.ANY)] + [vmem] * 6,
        out_specs=[vmem, vmem],
        out_shape=[block, block],
        scratch_shapes=[
            pltpu.VMEM((4, 2, depth, width), jnp.bfloat16),
            blocks(4), blocks(4), blocks(4), blocks(3), blocks(2),
            pltpu.VMEM((pad, width), jnp.bfloat16),
            floats(pad + rows, LANES), floats(groups, rows, LANES), floats(rows, LANES),
            floats(groups, CHUNKS, poles, LANES), floats(poles, width), floats(n, poles, width),
            dma((parts, 4, 2)), dma((4, parts)), dma((4, parts)),
            dma((3, parts)), dma((3, parts)), dma((2, parts)), dma((2, parts)), dma((parts,)),
            dma((parts,)), dma((parts,)), dma((n, parts)), dma((n, parts)),
        ],
        compiler_params=pltpu.CompilerParams(
            collective_id=2, has_side_effects=True, vmem_limit_bytes=58 * 1024 * 1024
        ),
        cost_estimate=pl.CostEstimate(
            flops=16 * rows * depth * width,
            bytes_accessed=16 * depth * width + 12 * rows * width,
            transcendentals=0,
        ),
    )(
        heads_out, residual_in, out_weight, gate_in, gate_out, short_taps, decay_rates, residues,
        skip_gain[None],
    )


def from_behind(value, axis, steps):
    count = lax.axis_size(axis)
    leading, last = (max(0, -steps), min(count, count - steps))
    return lax.ppermute(value, axis, [(source, source + steps) for source in range(leading, last)])


def attend(groups, key_rows, value_rows):
    width = key_rows.shape[1]
    heads = width // HD
    scale = HD ** (-0.5)
    query_sets = [(rows_q.reshape(rows_q.shape[0], heads, HD), pos_q) for rows_q, pos_q in groups]

    def update(state, queries, query_pos, keys_here, values_here, key_pos):
        running_top, running_total, running_sum = state
        scores = (
            jnp.einsum("qhd,khd->hqk", queries, keys_here, preferred_element_type=jnp.float32)
            * scale
        )
        allowed = (key_pos[None, :] <= query_pos[:, None])[None]
        masked = jnp.where(allowed, scores, masked_floor)
        new_top = jnp.maximum(running_top, jnp.max(masked, axis=-1))
        weights = jnp.where(allowed, jnp.exp(masked - new_top[..., None]), 0.0)
        rescale = jnp.exp(running_top - new_top)
        new_total = running_total * rescale + jnp.sum(weights, axis=-1)
        new_sum = running_sum * rescale[..., None] + jnp.einsum(
            "hqk,khd->hqd",
            weights.astype(jnp.bfloat16),
            values_here,
            preferred_element_type=jnp.float32,
        )
        return (new_top, new_total, new_sum)

    initial = tuple(
        (
            (
                jnp.full((heads, pos_q.shape[0]), masked_floor, jnp.float32),
                jnp.zeros((heads, pos_q.shape[0]), jnp.float32),
                jnp.zeros((heads, pos_q.shape[0], HD), jnp.float32),
            )
            for rows_q, pos_q in groups
        )
    )
    pieces = (
        lax.all_gather(key_rows, "ctx", axis=0, tiled=True),
        lax.all_gather(value_rows, "ctx", axis=0, tiled=True),
    )
    count = pieces[0].shape[0]
    blocks = count // count
    keys_all = pieces[0].reshape(blocks, count, heads, HD)
    values_all = pieces[1].reshape(blocks, count, heads, HD)
    index_rows = jnp.arange(count)
    pos_all = index_rows.reshape(blocks, count)

    def fold_step(states, block):
        keys_here, values_here, key_pos = block
        return (
            tuple(
                (
                    update(
                        states[g],
                        query_sets[g][0],
                        query_sets[g][1],
                        keys_here,
                        values_here,
                        key_pos,
                    )
                    for g in range(len(query_sets))
                )
            ),
            None,
        )

    result, _ = lax.scan(fold_step, initial, (keys_all, values_all, pos_all))
    return [(final[2] / final[1][..., None]).astype(jnp.bfloat16) for final in result]

def recurrence_states(signal_ref, rates_ref, ends_ref, state_ref):
    rows = signal_ref.shape[0]
    poles = rates_ref.shape[0]
    step = rows // CHUNKS
    decays = [
        jnp.broadcast_to(jnp.exp(-rates_ref[n : n + 1, :]), (CHUNKS, LANES)) for n in range(poles)
    ]

    def advance(i, states):
        piece = signal_ref[pl.ds(i, CHUNKS, stride=step), :]
        return tuple(decay * state + piece for decay, state in zip(decays, states))

    start = tuple(jnp.zeros((CHUNKS, LANES), jnp.float32) for _ in range(poles))
    ends = lax.fori_loop(0, step, advance, start, unroll=4)
    for n in range(poles):
        ends_ref[:, n, :] = ends[n]
    span = jnp.exp(-rates_ref[...] * float(step))
    total = jnp.zeros((poles, LANES), jnp.float32)
    for chunk in range(CHUNKS):
        total = span * total + ends_ref[chunk]
    state_ref[...] = total


def recurrence_outputs(signal_ref, rates_ref, residues_ref, ends_ref, before, conv_ref):
    rows = signal_ref.shape[0]
    poles = rates_ref.shape[0]
    step = rows // CHUNKS
    span = jnp.exp(-rates_ref[...] * float(step))
    for chunk in range(CHUNKS):
        here = ends_ref[chunk]
        ends_ref[chunk] = before
        before = span * before + here
    decays = [
        jnp.broadcast_to(jnp.exp(-rates_ref[n : n + 1, :]), (CHUNKS, LANES)) for n in range(poles)
    ]
    weights = [jnp.broadcast_to(residues_ref[n : n + 1, :], (CHUNKS, LANES)) for n in range(poles)]

    def advance(i, states):
        rows_here = pl.ds(i, CHUNKS, stride=step)
        piece = signal_ref[rows_here, :]
        states = tuple(decay * state + piece for decay, state in zip(decays, states))
        terms = [weight * state for weight, state in zip(weights, states)]
        while len(terms) > 1:
            terms = [sum(terms[i : i + 2][1:], terms[i]) for i in range(0, len(terms), 2)]
        conv_ref[rows_here, :] = terms[0]
        return states

    lax.fori_loop(0, step, advance, tuple(ends_ref[:, n, :] for n in range(poles)), unroll=2)


def make_signal(attended_ref, rim_ref, gate_ref, taps_ref, stream_ref, signal_ref):
    rows = attended_ref.shape[0]
    taps = taps_ref.shape[0]
    pad = rim_ref.shape[0]
    stream_ref[:pad, :] = rim_ref[...].astype(jnp.float32)
    stream_ref[pad:, :] = attended_ref[...].astype(jnp.float32)
    mixed = taps_ref[0:1, :] * stream_ref[pad : pad + rows, :]
    for tap in range(1, taps):
        mixed = mixed + taps_ref[tap : tap + 1, :] * stream_ref[pad - tap : pad - tap + rows, :]
    signal_ref[...] = gate_ref[...].astype(jnp.float32) * mixed


def states_kernel(attended_ref, rim_ref, gate_ref, taps_ref, rates_ref, signal_ref, ends_ref, state_ref, stream_ref):
    make_signal(attended_ref, rim_ref, gate_ref, taps_ref, stream_ref, signal_ref)
    recurrence_states(signal_ref, rates_ref, ends_ref, state_ref)


def outputs_kernel(signal_ref, ends_ref, before_ref, rates_ref, residues_ref, skip_ref, gate_ref, out_ref, held_ref, conv_ref):
    held_ref[...] = ends_ref[...]
    recurrence_outputs(signal_ref, rates_ref, residues_ref, held_ref, before_ref[...], conv_ref)
    mixed = conv_ref[...] + skip_ref[...] * signal_ref[...]
    out_ref[...] = (gate_ref[...].astype(jnp.float32) * mixed).astype(jnp.bfloat16)


def by_lanes(rows):
    return pl.BlockSpec((rows, LANES), lambda g: (0, g))


def hyena(attended, gate_in, gate_out, short_taps, decay_rates, residues, skip_gain):
    rows, width = attended.shape
    taps = short_taps.shape[0]
    poles = decay_rates.shape[0]
    segment = lax.axis_index("ctx")
    groups = width // LANES
    pad = 16
    rim = from_behind(attended[rows - pad :], "ctx", 1)
    ends_spec = pl.BlockSpec((CHUNKS, poles, LANES), lambda g: (0, 0, g))
    signal, ends, state = pl.pallas_call(
        states_kernel,
        grid=(groups,),
        in_specs=[by_lanes(rows), by_lanes(pad), by_lanes(rows), by_lanes(taps), by_lanes(poles)],
        out_specs=[by_lanes(rows), ends_spec, by_lanes(poles)],
        out_shape=[
            jax.ShapeDtypeStruct((rows, width), jnp.float32),
            jax.ShapeDtypeStruct((CHUNKS, poles, width), jnp.float32),
            jax.ShapeDtypeStruct((poles, width), jnp.float32),
        ],
        scratch_shapes=[pltpu.VMEM((pad + rows, LANES), jnp.float32)],
    )(attended, rim, gate_in, short_taps, decay_rates)
    states = lax.all_gather(state, "ctx", axis=0)
    earlier = jnp.arange(states.shape[0])
    gap = jnp.maximum((segment - earlier - 1) * rows, 0).astype(jnp.float32)
    factor = jnp.where(
        (earlier < segment)[:, None, None], jnp.exp(-decay_rates[None] * gap[:, None, None]), 0.0
    )
    before = jnp.sum(factor * states, axis=0)
    return pl.pallas_call(
        outputs_kernel,
        grid=(groups,),
        in_specs=[
            by_lanes(rows), ends_spec, by_lanes(poles), by_lanes(poles), by_lanes(poles), by_lanes(1), by_lanes(rows),
        ],
        out_specs=by_lanes(rows),
        out_shape=jax.ShapeDtypeStruct((rows, width), jnp.bfloat16),
        scratch_shapes=[
            pltpu.VMEM((CHUNKS, poles, LANES), jnp.float32),
            pltpu.VMEM((rows, LANES), jnp.float32),
        ],
    )(signal, ends, before, decay_rates, residues, skip_gain[None], gate_out)


def per_device(
    residual_in,
    query_rows,
    key_rows,
    value_rows,
    out_weight,
    gate_in,
    gate_out,
    short_taps,
    decay_rates,
    residues,
    skip_gain,
):
    rows, width = residual_in.shape
    segments = lax.axis_size("ctx")
    heads = width // HD
    if heads % segments == 0:
        heads_out = spread_attention(query_rows, key_rows, value_rows)
    else:
        query_pos = lax.axis_index("ctx") * rows + jnp.arange(rows)
        heads_out = attend([(query_rows, query_pos)], key_rows, value_rows)[0]
        heads_out = heads_out.transpose(1, 0, 2).reshape(rows, width)
    if lax.axis_size("mp") == 8:
        return tuple(
            project_hyena(
                heads_out, residual_in, out_weight, gate_in, gate_out, short_taps, decay_rates,
                residues, skip_gain,
            )
        )
    partial = jnp.einsum(
        "qk,kc->cq", heads_out, out_weight, preferred_element_type=jnp.float32
    ).astype(jnp.bfloat16)
    projected = lax.psum_scatter(partial, "mp", scatter_dimension=0, tiled=True)
    attended = (
        residual_in.astype(jnp.float32) + projected.astype(jnp.float32).T
    ).astype(jnp.bfloat16)
    hyena_out = hyena(attended, gate_in, gate_out, short_taps, decay_rates, residues, skip_gain)
    return (attended, hyena_out)


def solution(mesh):
    in_specs = (
        P("ctx", "mp"),
        P("ctx", "mp"),
        P("ctx", "mp"),
        P("ctx", "mp"),
        P("mp", None),
        P("ctx", "mp"),
        P("ctx", "mp"),
        P(None, "mp"),
        P(None, "mp"),
        P(None, "mp"),
        P("mp"),
    )
    out_specs = (P("ctx", "mp"), P("ctx", "mp"))
    return jax.shard_map(
        per_device, mesh=mesh, in_specs=in_specs, out_specs=out_specs, check_vma=False
    )
```
